256 devices in a mesh: day: 8 (over y, z_lo), sta: 32 (over z_hi, x, core).
Axes of the slice: x: 4, y: 4, z: 8 (z_hi: 4, z_lo: 2; z = z_hi * 2 + z_lo), core: 2. Of those that a mesh axis runs over, the one named last changes fastest.
Arguments:
- spectra: bfloat16 [8, 512, 8, 2, 3584], P('day', 'sta'), may hold values from -1600 to 1600, as said below
- hour_flags: int32 [8, 512, 8], P('day', 'sta'), may hold values 0 or 1
- sources: int32 [2, 8], replicated, may hold values from 0 to 511
- station_rows: int32 [512], replicated, may hold values from 0 to 511, each once
Outputs:
- stacked: float32 [16, 512, 1024], P(None, 'sta', 'day')
The draws below stay inside these ranges and needn't reach their ends.
Inputs may be any that keep to these rules, and one draw needn't show every extreme that they name: `spectra`: spectral values.
All inputs are finite; a program needn't handle non-finite values. No bound on the sum of `hour_flags` on one device may be relied on, other than what follows from the above.
Results may differ from the reference program's by a relative error of at most 0.0034.
Values may be sent and summed in bfloat16 or wider, within the bound.
A program may use at most 128 MiB of HBM per device.

```python
import jax
import jax.numpy as jnp
from jax import lax

HOURS = 8
BINS = 3584
LAGS = 1024
SRC = 8
ROUNDS = 2
DAYS = 8
STATIONS = 512
SOURCES = 16


def draw_spectra(key, part):
    key = jax.random.fold_in(key, 11)
    key_noise, key_common, key_rows, key_share, key_dead = jax.random.split(key, 5)
    shape = (DAYS, STATIONS, HOURS, 2, BINS)
    common_shape = (DAYS, 1, HOURS, 2, BINS)
    noise = jnp.clip(jax.random.normal(key_noise, shape, jnp.float32), -5.0, 5.0)
    common = jnp.clip(jax.random.normal(key_common, common_shape, jnp.float32), -5.0, 5.0)
    spread = jnp.log(10.0)
    share = jax.random.uniform(key_share, (DAYS, 1, 1, 1, BINS), jnp.float32, 0.0, 1.0)
    mixed = jnp.sqrt(2.0 * (1.0 - share)) * noise + jnp.sqrt(share) * common
    row_scale = jnp.exp(jax.random.uniform(key_rows, (DAYS, STATIONS, HOURS, 1, 1), jnp.float32) * spread)
    live = (jax.random.randint(key_dead, (DAYS, STATIONS, HOURS, 1, 1), 0, 4) > 0).astype(jnp.float32)
    return (mixed * row_scale * live).astype(jnp.bfloat16)


def place_ends(entries, key, smallest, largest):
    shape = entries.shape
    place = [jax.random.randint(jax.random.fold_in(key, axis), (), 0, shape[axis]) for axis in range(len(shape))]
    entries = entries.at[tuple(place)].set(smallest)
    longest = shape.index(max(shape))
    place[longest] = (place[longest] + 1) % shape[longest]
    return entries.at[tuple(place)].set(largest)


def setup_inputs(seed: int = 0) -> dict:
    key_list = jax.random.split(jax.random.key(seed), 5)
    spectra = draw_spectra(jax.random.fold_in(key_list[4], 71), 0)
    hour_flags = place_ends((jax.random.randint(key_list[1], (DAYS, STATIONS, HOURS), 0, 4) < 3).astype(jnp.int32), jax.random.fold_in(key_list[1], 1), 0, 1)
    sources = place_ends(jax.random.randint(key_list[2], (ROUNDS, SRC), 0, STATIONS), jax.random.fold_in(key_list[2], 1), 0, STATIONS - 1).astype(jnp.int32)
    station_rows = jax.random.permutation(key_list[3], STATIONS).astype(jnp.int32)
    return dict(spectra=spectra, hour_flags=hour_flags, sources=sources, station_rows=station_rows)


EPSILON = 1e-06

def reference(spectra, hour_flags, sources, station_rows):
    source_rows = station_rows[sources.reshape(-1)]
    cosine_total = jnp.zeros((SOURCES, STATIONS, BINS), jnp.float32)
    sine_total = jnp.zeros((SOURCES, STATIONS, BINS), jnp.float32)
    for day_index in range(DAYS):
        values = spectra[day_index].astype(jnp.float32)
        power_mean = lax.optimization_barrier(jnp.mean(values * values, axis=(2, 3)))
        valid = hour_flags[day_index].astype(jnp.float32)
        whitened = (values * (valid / jnp.sqrt(power_mean + EPSILON))[:, :, None, None]).astype(jnp.bfloat16)
        receiver = whitened.astype(jnp.float32)
        source_spec = receiver[source_rows]
        source_valid = valid[source_rows]
        intersection = jnp.dot(source_valid, valid.T, precision=lax.Precision.HIGHEST)
        weights = 1.0 / jnp.maximum(intersection, 1.0)
        cosine_sum = jnp.zeros((SOURCES, STATIONS, BINS), jnp.float32)
        sine_sum = jnp.zeros((SOURCES, STATIONS, BINS), jnp.float32)
        for hour_index in range(HOURS):
            first_a = source_spec[:, None, hour_index, 0]
            first_b = source_spec[:, None, hour_index, 1]
            second_c = receiver[None, :, hour_index, 0]
            second_e = receiver[None, :, hour_index, 1]
            cosine_sum = cosine_sum + first_a * second_c + first_b * second_e
            sine_sum = sine_sum + first_b * second_c - first_a * second_e
        cosine_total = cosine_total + cosine_sum * weights[:, :, None]
        sine_total = sine_total + sine_sum * weights[:, :, None]
    complex_spec = cosine_total + 1j * sine_total
    padded = jnp.concatenate([complex_spec, jnp.zeros_like(complex_spec)], axis=-1)
    series = jnp.fft.ifft(padded, axis=-1) * (2 * BINS)
    lag_index = jnp.mod(jnp.arange(LAGS, dtype=jnp.int32) - LAGS // 2, 2 * BINS).astype(jnp.int32)
    picked = jnp.real(jnp.take(series, lag_index, axis=-1))
    return (picked / jnp.sqrt(jnp.float32(BINS))).astype(jnp.float32)
```

```python
import functools
import math

import jax
import jax.numpy as jnp
import ml_dtypes
import numpy as np
from jax import lax
from jax.experimental import pallas as pl
from jax.experimental.pallas import tpu as pltpu
from jax.sharding import PartitionSpec as P

BINS = 3584
LAGS = 1024
HALF = LAGS // 2
QUARTER = BINS // 4
EPSILON = 1e-06
SLOTS = 4
MESH = pl.DeviceIdType.MESH
BF16 = jnp.bfloat16
F32 = jnp.float32


def tables():
    bins = np.arange(BINS, dtype=np.int64)[:, None]
    half_lags = 2 * np.arange(HALF, dtype=np.int64)[None] + 1
    angles = np.pi * ((bins * half_lags) % (4 * BINS)) / (2 * BINS)
    table = np.concatenate([np.cos(angles), np.sin(angles)], 1).astype(ml_dtypes.bfloat16)
    shift = np.pi * np.arange(BINS) / (2 * BINS)
    turn = np.stack([np.cos(shift), np.sin(shift)]).astype(np.float32)
    mirror = np.eye(HALF)[::-1].astype(ml_dtypes.bfloat16)
    return table, turn, mirror


def mult(value, k):
    return pl.multiple_of(value, k)


def gather_kernel(sources, rows_ref, white, out, slots, recv, picked, twin, src, s_sc, r_sc, s_tw, r_tw,
                  s_z, r_z, s_x, r_x, s_t, r_t):
    day = lax.axis_index("day")
    me = lax.axis_index("sta")
    z, x, c, chip = me // 8, (me // 2) % 4, me % 2, me // 2

    def dev(z_to, x_to, c_to):
        return (day, z_to * 8 + x_to * 2 + c_to)

    offsets = [(dz, dx) for dz in (2, 1, 3, 0) for dx in (2, 1, 3, 0) if (dz, dx) != (0, 0)]
    barrier = pltpu.get_barrier_semaphore()
    for dz, dx in offsets:
        pl.semaphore_signal(barrier, inc=1, device_id=dev((z + dz) % 4, (x + dx) % 4, c), device_id_type=MESH)
    pl.semaphore_signal(barrier, inc=1, device_id=dev(z, x, 1 - c), device_id_type=MESH)

    holder, local, rank = [], [], []
    for i in range(16):
        row = rows_ref[sources[i // 8, i % 8]]
        holder.append(row // 16)
        local.append(row % 16)
        count = jnp.int32(0)
        for j in range(i):
            count = count + jnp.where(holder[j] == holder[i], 1, 0)
        rank.append(count)
    ri = lax.broadcasted_iota(jnp.int32, (64, 256), 0)
    ci = lax.broadcasted_iota(jnp.int32, (64, 256), 1)
    target = jnp.full((64, 256), -1, jnp.int32)
    base = 128 * ((ri // 8) % 2) + 32 * (ri // 16) + 16 * ((ri // 4) % 2)
    for i in range(16):
        key = jnp.where(holder[i] == me, rank[i], 99)
        target = jnp.where(ri % 4 == key, base + local[i], target)
    pick = jnp.where(ci == target, 1.0, 0.0).astype(BF16)
    slots[...] = jnp.dot(pick, white[...], preferred_element_type=F32).astype(BF16)
    pl.semaphore_wait(barrier, 16)

    copies = []
    for n, (dz, dx) in enumerate(offsets):
        z_to, x_to = (z + dz) % 4, (x + dx) % 4
        copy = pltpu.make_async_remote_copy(
            src_ref=slots.at[pl.ds(mult(16 * z_to, 16), 16), pl.ds(mult(QUARTER * x_to, 128), QUARTER)],
            dst_ref=recv.at[pl.ds(mult(16 * chip, 16), 16)],
            send_sem=s_sc.at[n],
            recv_sem=r_sc.at[n],
            device_id=dev(z_to, x_to, c),
            device_id_type=MESH,
        )
        copy.start()
        copies.append(copy)
    own = (pl.ds(mult(16 * z, 16), 16), pl.ds(mult(QUARTER * x, 128), QUARTER))
    recv[pl.ds(mult(16 * chip, 16), 16), :] = slots[own]
    target = jnp.full((64, 256), -1, jnp.int32)
    for i in range(16):
        where = jnp.where(holder[i] % 2 == c, 16 * (holder[i] // 2) + rank[i], -1000)
        target = jnp.where(ri % 16 == i, where + 8 * (ri // 32) + 4 * ((ri // 16) % 2), target)
    pick = jnp.where(ci == target, 1.0, 0.0).astype(BF16)
    for copy in copies:
        copy.wait()
    picked[...] = jnp.dot(pick, recv[...], preferred_element_type=F32).astype(BF16)
    copy = pltpu.make_async_remote_copy(
        src_ref=picked.at[pl.ds(mult(32 * (1 - c), 32), 32)],
        dst_ref=twin,
        send_sem=s_tw,
        recv_sem=r_tw,
        device_id=dev(z, x, 1 - c),
        device_id_type=MESH,
    )
    copy.start()
    copy.wait()

    def piece(z_of, x_of):
        return src.at[pl.ds(mult(128 * c + 32 * z_of, 32), 32), pl.ds(mult(QUARTER * x_of, 128), QUARTER)]

    def half(x_of):
        return src.at[pl.ds(mult(128 * c, 128), 128), pl.ds(mult(QUARTER * x_of, 128), QUARTER)]

    def send(ref, s_sem, r_sem, target_id):
        copy = pltpu.make_async_remote_copy(
            src_ref=ref, dst_ref=ref, send_sem=s_sem, recv_sem=r_sem, device_id=target_id, device_id_type=MESH
        )
        copy.start()
        return copy

    piece(z, x)[...] = picked[pl.ds(mult(32 * c, 32), 32), :] + twin[...]

    def send_x(k, z_of):
        return [
            send(piece(z_of, x), s_x.at[k, n], r_x.at[k, n], dev(z, (x + dx) % 4, c))
            for n, dx in enumerate((2, 1, 3))
        ]

    along_z = [send(piece(z, x), s_z.at[n], r_z.at[n], dev((z + dz) % 4, x, c)) for n, dz in enumerate((2, 1, 3))]
    along_x = [send_x(0, z)]
    for n, dz in ((1, 1), (2, 3), (0, 2)):
        along_z[n].wait()
        along_x.append(send_x(1 + n, (z + 4 - dz) % 4))
    across = [send(half(x), s_t.at[0], r_t.at[0], dev(z, x, 1 - c))]
    for n, dx in ((1, 1), (2, 3), (0, 2)):
        for k in range(4):
            along_x[k][n].wait()
        across.append(send(half((x + 4 - dx) % 4), s_t.at[1 + n], r_t.at[1 + n], dev(z, x, 1 - c)))
    for copy in across:
        copy.wait()
    out[...] = src[...]


def gather_sources(sources, station_rows, white):
    sem = pltpu.SemaphoreType.DMA
    return pl.pallas_call(
        gather_kernel,
        out_shape=jax.ShapeDtypeStruct((256, BINS), BF16),
        in_specs=[pl.BlockSpec(memory_space=pltpu.SMEM)] * 2 + [pl.BlockSpec(memory_space=pltpu.VMEM)],
        out_specs=pl.BlockSpec(memory_space=pltpu.VMEM),
        scratch_shapes=[
            pltpu.VMEM((64, BINS), BF16),
            pltpu.VMEM((256, QUARTER), BF16),
            pltpu.VMEM((64, QUARTER), BF16),
            pltpu.VMEM((32, QUARTER), BF16),
            pltpu.VMEM((256, BINS), BF16),
            sem((15,)), sem((15,)), sem, sem, sem((3,)), sem((3,)), sem((4, 3)), sem((4, 3)), sem((4,)), sem((4,)),
        ],
        compiler_params=pltpu.CompilerParams(collective_id=0, has_side_effects=True, vmem_limit_bytes=48 << 20),
    )(sources, station_rows, white)


def correlate_kernel(white, src, table, turn, mirror, weights, out, cross, total, rec_f, src_f):
    step = pl.program_id(0)
    tiles = white.shape[1] // 128

    @pl.when(step == 0)
    def _():
        total[...] = jnp.zeros_like(total)

    for t in range(tiles):
        lanes = pl.ds(t * 128, 128)
        co, si = turn[0:1, lanes], turn[1:2, lanes]
        for h in range(8):
            c = white[pl.ds(32 * h, 16), lanes].astype(F32)
            e = white[pl.ds(32 * h + 16, 16), lanes].astype(F32)
            rec_f[t, h, 0], rec_f[t, h, 1], rec_f[t, h, 2] = c, c - e, c + e
            a = src[pl.ds(32 * h, 16), lanes].astype(F32)
            b = src[pl.ds(32 * h + 16, 16), lanes].astype(F32)
            a_turn, b_turn = a * co + b * si, b * co - a * si
            src_f[t, h, 0], src_f[t, h, 1], src_f[t, h, 2] = a_turn + b_turn, b_turn, a_turn
    for t in range(tiles):
        lanes = pl.ds(t * 128, 128)
        for block in range(4):
            sums = [[None] * 3 for _ in range(4)]
            for h in range(8):
                rec = [rec_f[t, h, k] for k in range(3)]
                for n in range(4):
                    for k in range(3):
                        row = src_f[t, h, k, pl.ds(block * 4 + n, 1), :]
                        term = jnp.broadcast_to(row, (16, 128)) * rec[k]
                        sums[n][k] = term if h == 0 else sums[n][k] + term
            for n in range(4):
                rows = pl.ds(16 * (block * 4 + n), 16)
                cross[0, rows, lanes] = (sums[n][0] - sums[n][1]).astype(BF16)
                cross[1, rows, lanes] = (sums[n][0] - sums[n][2]).astype(BF16)
    total[0] += jnp.dot(cross[0], table[:, 0:HALF], preferred_element_type=F32)
    total[1] += jnp.dot(cross[1], table[:, HALF:], preferred_element_type=F32)

    @pl.when(step == pl.num_programs(0) - 1)
    def _():
        scale = weights[...]
        even, odd = total[0] * scale, total[1] * scale
        out[:, HALF:] = (even - odd).astype(BF16)
        back = jnp.dot((even + odd).astype(BF16), mirror[...], preferred_element_type=F32)
        out[:, 0:HALF] = back.astype(BF16)


def correlate(white, src, weights):
    table, turn, mirror = tables()
    width = QUARTER
    return pl.pallas_call(
        correlate_kernel,
        grid=(BINS // width,),
        out_shape=jax.ShapeDtypeStruct((256, LAGS), BF16),
        in_specs=[
            pl.BlockSpec((256, width), lambda q: (0, q)),
            pl.BlockSpec((256, width), lambda q: (0, q)),
            pl.BlockSpec((width, LAGS), lambda q: (q, 0)),
            pl.BlockSpec((2, width), lambda q: (0, q)),
            pl.BlockSpec((HALF, HALF), lambda q: (0, 0)),
            pl.BlockSpec((256, 1), lambda q: (0, 0)),
        ],
        out_specs=pl.BlockSpec((256, LAGS), lambda q: (0, 0)),
        scratch_shapes=[
            pltpu.VMEM((2, 256, width), BF16),
            pltpu.VMEM((2, 256, HALF), F32),
            pltpu.VMEM((width // 128, 8, 3, 16, 128), F32),
            pltpu.VMEM((width // 128, 8, 3, 16, 128), F32),
        ],
        compiler_params=pltpu.CompilerParams(vmem_limit_bytes=48 << 20),
    )(white, src, jnp.asarray(table), jnp.asarray(turn), jnp.asarray(mirror), weights)


def stack_kernel(term, out, recv, s_sem, r_sem):
    day = lax.axis_index("day")
    sta = lax.axis_index("sta")
    barrier = pltpu.get_barrier_semaphore()
    for n in range(1, 8):
        pl.semaphore_signal(barrier, inc=1, device_id=((day + n) % 8, sta), device_id_type=MESH)
    pl.semaphore_wait(barrier, 7)
    copies = []
    for n in range(1, 8):
        to = (day + n) % 8
        copy = pltpu.make_async_remote_copy(
            src_ref=term.at[:, pl.ds(mult(128 * to, 128), 128)],
            dst_ref=recv.at[n - 1],
            send_sem=s_sem.at[n - 1],
            recv_sem=r_sem.at[n - 1],
            device_id=(to, sta),
            device_id_type=MESH,
        )
        copy.start()
        copies.append(copy)
    for copy in copies:
        copy.wait()
    total = term[:, pl.ds(mult(128 * day, 128), 128)].astype(F32)
    for n in range(7):
        total = total + recv[n].astype(F32)
    out[...] = total


def stack_days(term):
    sem = pltpu.SemaphoreType.DMA
    return pl.pallas_call(
        stack_kernel,
        out_shape=jax.ShapeDtypeStruct((256, 128), F32),
        in_specs=[pl.BlockSpec(memory_space=pltpu.VMEM)],
        out_specs=pl.BlockSpec(memory_space=pltpu.VMEM),
        scratch_shapes=[pltpu.VMEM((7, 256, 128), BF16), sem((7,)), sem((7,))],
        compiler_params=pltpu.CompilerParams(collective_id=1, has_side_effects=True, vmem_limit_bytes=16 << 20),
    )(term)


def shards(spectra, hour_flags, sources, station_rows):
    me = lax.axis_index("sta")
    values = spectra[0].astype(F32)
    power = jnp.mean(values * values, axis=(2, 3))
    valid = hour_flags[0].astype(F32)
    white = (values * (valid / jnp.sqrt(power + EPSILON))[:, :, None, None]).astype(BF16)
    white = white.reshape(16, 4, 2, 2, BINS).transpose(2, 1, 3, 0, 4).reshape(256, BINS)

    rows = station_rows[sources.reshape(-1)]
    holder, local = rows // 16, rows % 16
    mine = (holder == me)[:, None]
    source_valid = lax.psum(jnp.where(mine, valid[local], 0.0), "sta")
    shared = jnp.dot(source_valid, valid.T, precision=lax.Precision.HIGHEST)
    weights = (1.0 / jnp.maximum(shared, 1.0)).reshape(256, 1) * (1.0 / math.sqrt(BINS))

    def general(white):
        kept = jnp.where(mine, white.reshape(16, 16, BINS)[:, local], 0).astype(BF16)
        return lax.psum(kept.reshape(256, BINS), "sta")

    def spread(white):
        return gather_sources(sources, station_rows, white)

    load = jnp.max(jnp.sum((holder[:, None] == holder[None, :]).astype(jnp.int32), axis=1))
    src = lax.cond(load <= SLOTS, spread, general, white)
    term = correlate(white, src, weights)
    return stack_days(term).reshape(16, 16, 128)


def solution(mesh):
    in_specs = (P("day", "sta", None, None, None), P("day", "sta", None), P(), P())
    out_specs = P(None, "sta", "day")
    return jax.shard_map(shards, mesh=mesh, in_specs=in_specs, out_specs=out_specs, check_vma=False)
```

```python
import functools
import math

import jax
import jax.numpy as jnp
import ml_dtypes
import numpy as np
from jax import lax
from jax.experimental import pallas as pl
from jax.experimental.pallas import tpu as pltpu
from jax.sharding import PartitionSpec as P

BINS = 3584
LAGS = 1024
HALF = LAGS // 2
QUARTER = BINS // 4
EPSILON = 1e-06
SLOTS = 4
MESH = pl.DeviceIdType.MESH
BF16 = jnp.bfloat16
F32 = jnp.float32


def tables():
    bins = np.arange(BINS, dtype=np.int64)[:, None]
    half_lags = 2 * np.arange(HALF, dtype=np.int64)[None] + 1
    angles = np.pi * ((bins * half_lags) % (4 * BINS)) / (2 * BINS)
    table = np.concatenate([np.cos(angles), np.sin(angles)], 1).astype(ml_dtypes.bfloat16)
    shift = np.pi * np.arange(BINS) / (2 * BINS)
    turn = np.stack([np.cos(shift), np.sin(shift)]).astype(np.float32)
    mirror = np.eye(HALF)[::-1].astype(ml_dtypes.bfloat16)
    return table, turn, mirror


def mult(value, k):
    return pl.multiple_of(value, k)


def correlate_kernel(white, src, table, turn, mirror, weights, out, cross, total, rec_f, src_f):
    step = pl.program_id(0)
    tiles = white.shape[1] // 128

    @pl.when(step == 0)
    def _():
        total[...] = jnp.zeros_like(total)

    for t in range(tiles):
        lanes = pl.ds(t * 128, 128)
        co, si = turn[0:1, lanes], turn[1:2, lanes]
        for h in range(8):
            c = white[pl.ds(32 * h, 16), lanes].astype(F32)
            e = white[pl.ds(32 * h + 16, 16), lanes].astype(F32)
            rec_f[t, h, 0], rec_f[t, h, 1], rec_f[t, h, 2] = c, c - e, c + e
            a = src[pl.ds(32 * h, 16), lanes].astype(F32)
            b = src[pl.ds(32 * h + 16, 16), lanes].astype(F32)
            a_turn, b_turn = a * co + b * si, b * co - a * si
            src_f[t, h, 0], src_f[t, h, 1], src_f[t, h, 2] = a_turn + b_turn, b_turn, a_turn
    for t in range(tiles):
        lanes = pl.ds(t * 128, 128)
        for block in range(4):
            sums = [[None] * 3 for _ in range(4)]
            for h in range(8):
                rec = [rec_f[t, h, k] for k in range(3)]
                for n in range(4):
                    for k in range(3):
                        row = src_f[t, h, k, pl.ds(block * 4 + n, 1), :]
                        term = jnp.broadcast_to(row, (16, 128)) * rec[k]
                        sums[n][k] = term if h == 0 else sums[n][k] + term
            for n in range(4):
                rows = pl.ds(16 * (block * 4 + n), 16)
                cross[0, rows, lanes] = (sums[n][0] - sums[n][1]).astype(BF16)
                cross[1, rows, lanes] = (sums[n][0] - sums[n][2]).astype(BF16)
    total[0] += jnp.dot(cross[0], table[:, 0:HALF], preferred_element_type=F32)
    total[1] += jnp.dot(cross[1], table[:, HALF:], preferred_element_type=F32)

    @pl.when(step == pl.num_programs(0) - 1)
    def _():
        scale = weights[...]
        even, odd = total[0] * scale, total[1] * scale
        out[:, HALF:] = (even - odd).astype(BF16)
        back = jnp.dot((even + odd).astype(BF16), mirror[...], preferred_element_type=F32)
        out[:, 0:HALF] = back.astype(BF16)


def correlate(white, src, weights):
    table, turn, mirror = tables()
    width = QUARTER
    return pl.pallas_call(
        correlate_kernel,
        grid=(BINS // width,),
        out_shape=jax.ShapeDtypeStruct((256, LAGS), BF16),
        in_specs=[
            pl.BlockSpec((256, width), lambda q: (0, q)),
            pl.BlockSpec((256, width), lambda q: (0, q)),
            pl.BlockSpec((width, LAGS), lambda q: (q, 0)),
            pl.BlockSpec((2, width), lambda q: (0, q)),
            pl.BlockSpec((HALF, HALF), lambda q: (0, 0)),
            pl.BlockSpec((256, 1), lambda q: (0, 0)),
        ],
        out_specs=pl.BlockSpec((256, LAGS), lambda q: (0, 0)),
        scratch_shapes=[
            pltpu.VMEM((2, 256, width), BF16),
            pltpu.VMEM((2, 256, HALF), F32),
            pltpu.VMEM((width // 128, 8, 3, 16, 128), F32),
            pltpu.VMEM((width // 128, 8, 3, 16, 128), F32),
        ],
        compiler_params=pltpu.CompilerParams(vmem_limit_bytes=48 << 20),
    )(white, src, jnp.asarray(table), jnp.asarray(turn), jnp.asarray(mirror), weights)


def fused_kernel(sources, rows_ref, spectra, flags, table_hbm, turn, mirror, out, load, table, white, slots, recv, picked,
                 twin, src, valid, cross, total, rec_f, src_f, days, daily, s_tab, s_sc, r_sc, s_tw, r_tw, s_z, r_z,
                 s_x, r_x, s_t, r_t, s_fz, r_fz, s_fx, r_fx, s_ft, r_ft, s_d, r_d):
    day = lax.axis_index("day")
    me = lax.axis_index("sta")
    z, x, c, chip = me // 8, (me // 2) % 4, me % 2, me // 2

    def dev(z_to, x_to, c_to):
        return (day, z_to * 8 + x_to * 2 + c_to)

    def remote(source, target, s_sem, r_sem, device):
        copy = pltpu.make_async_remote_copy(
            src_ref=source, dst_ref=target, send_sem=s_sem, recv_sem=r_sem, device_id=device, device_id_type=MESH
        )
        copy.start()
        return copy

    offsets = [(dz, dx) for dz in (2, 1, 3, 0) for dx in (2, 1, 3, 0) if (dz, dx) != (0, 0)]
    barrier = pltpu.get_barrier_semaphore()
    for dz, dx in offsets:
        pl.semaphore_signal(barrier, inc=1, device_id=dev((z + dz) % 4, (x + dx) % 4, c), device_id_type=MESH)
    pl.semaphore_signal(barrier, inc=1, device_id=dev(z, x, 1 - c), device_id_type=MESH)
    for n in range(1, 8):
        pl.semaphore_signal(barrier, inc=1, device_id=((day + n) % 8, me), device_id_type=MESH)
    table_copy = pltpu.make_async_copy(table_hbm, table, s_tab)
    table_copy.start()

    ri = lax.broadcasted_iota(jnp.int32, (256, 256), 0)
    ci = lax.broadcasted_iota(jnp.int32, (256, 256), 1)
    natural = (ri % 16) * 16 + 4 * ((ri // 32) % 4) + 2 * (ri // 128) + (ri // 16) % 2
    order = jnp.where(ci == natural, 1.0, 0.0).astype(BF16)
    power = jnp.zeros((256, 128), F32)
    for k in range(BINS // 256):
        lanes = pl.ds(256 * k, 256)
        values = jnp.dot(order, spectra[:, lanes], preferred_element_type=F32)
        white[:, lanes] = values.astype(BF16)
        squares = values * values
        power = power + squares[:, :128] + squares[:, 128:]
    power = jnp.sum(power, axis=1, keepdims=True)
    flag = flags[...].astype(F32)
    for h in range(8):
        hour = 2 * (h % 4) + h // 4
        mean = (power[32 * h:32 * h + 16] + power[32 * h + 16:32 * h + 32]) * (1.0 / (2 * BINS))
        scale = flag[:, hour:hour + 1] / jnp.sqrt(mean + EPSILON)
        for p in range(2):
            rows = pl.ds(32 * h + 16 * p, 16)
            white[rows, :] = (white[rows, :].astype(F32) * scale).astype(BF16)
    wide = jnp.concatenate([flag, jnp.zeros((16, 120), F32)], axis=1)
    own_flags = pl.ds(mult(256 * c + 64 * x + 16 * z, 16), 16)
    valid[own_flags, :] = wide.astype(BF16)

    holder, local, rank = [], [], []
    most = jnp.int32(0)
    for i in range(16):
        row = rows_ref[sources[i // 8, i % 8]]
        holder.append(row // 16)
        local.append(row % 16)
        count = jnp.int32(0)
        for j in range(i):
            count = count + jnp.where(holder[j] == holder[i], 1, 0)
        rank.append(count)
        most = jnp.maximum(most, count + 1)
    load[0] = most
    ri, ci = ri[:64], ci[:64]
    target = jnp.full((64, 256), -1, jnp.int32)
    base = 128 * ((ri // 8) % 2) + 32 * (ri // 16) + 16 * ((ri // 4) % 2)
    for i in range(16):
        key = jnp.where(holder[i] == me, rank[i], 99)
        target = jnp.where(ri % 4 == key, base + local[i], target)
    pick = jnp.where(ci == target, 1.0, 0.0).astype(BF16)
    slots[...] = jnp.dot(pick, white[...], preferred_element_type=F32).astype(BF16)
    pl.semaphore_wait(barrier, 23)

    copies = []
    for n, (dz, dx) in enumerate(offsets):
        z_to, x_to = (z + dz) % 4, (x + dx) % 4
        copies.append(
            remote(
                slots.at[pl.ds(mult(16 * z_to, 16), 16), pl.ds(mult(QUARTER * x_to, 128), QUARTER)],
                recv.at[pl.ds(mult(16 * chip, 16), 16)],
                s_sc.at[n],
                r_sc.at[n],
                dev(z_to, x_to, c),
            )
        )
    ref = valid.at[own_flags]
    flag_z = [remote(ref, ref, s_fz.at[n], r_fz.at[n], dev((z + 1 + n) % 4, x, c)) for n in range(3)]
    recv[pl.ds(mult(16 * chip, 16), 16), :] = slots[
        pl.ds(mult(16 * z, 16), 16), pl.ds(mult(QUARTER * x, 128), QUARTER)
    ]
    target = jnp.full((64, 256), -1, jnp.int32)
    for i in range(16):
        where = jnp.where(holder[i] % 2 == c, 16 * (holder[i] // 2) + rank[i], -1000)
        target = jnp.where(ri % 16 == i, where + 8 * (ri // 32) + 4 * ((ri // 16) % 2), target)
    pick = jnp.where(ci == target, 1.0, 0.0).astype(BF16)

    def receiver_planes(t, carry):
        lanes = pl.ds(mult(t * 128, 128), 128)
        for h in range(8):
            cosine = white[pl.ds(32 * h, 16), lanes].astype(F32)
            sine = white[pl.ds(32 * h + 16, 16), lanes].astype(F32)
            rec_f[t, h, 0] = cosine
            rec_f[t, h, 1] = cosine - sine
            rec_f[t, h, 2] = cosine + sine
        return carry

    lax.fori_loop(0, BINS // 128, receiver_planes, 0)
    total[...] = jnp.zeros_like(total)

    for copy in flag_z:
        copy.wait()
    ref = valid.at[pl.ds(mult(256 * c + 64 * x, 64), 64)]
    flag_x = [remote(ref, ref, s_fx.at[n], r_fx.at[n], dev(z, (x + 1 + n) % 4, c)) for n in range(3)]
    for copy in copies:
        copy.wait()
    picked[...] = jnp.dot(pick, recv[...], preferred_element_type=F32).astype(BF16)
    copy = remote(picked.at[pl.ds(mult(32 * (1 - c), 32), 32)], twin, s_tw, r_tw, dev(z, x, 1 - c))
    copy.wait()

    def piece(z_of, x_of):
        return src.at[pl.ds(mult(128 * c + 32 * z_of, 32), 32), pl.ds(mult(QUARTER * x_of, 128), QUARTER)]

    def half(x_of):
        return src.at[pl.ds(mult(128 * c, 128), 128), pl.ds(mult(QUARTER * x_of, 128), QUARTER)]

    def send(ref, s_sem, r_sem, device):
        return remote(ref, ref, s_sem, r_sem, device)

    piece(z, x)[...] = picked[pl.ds(mult(32 * c, 32), 32), :] + twin[...]

    def send_x(k, z_of):
        return [
            send(piece(z_of, x), s_x.at[k, n], r_x.at[k, n], dev(z, (x + dx) % 4, c))
            for n, dx in enumerate((2, 1, 3))
        ]

    along_z = [send(piece(z, x), s_z.at[n], r_z.at[n], dev((z + dz) % 4, x, c)) for n, dz in enumerate((2, 1, 3))]
    along_x = [send_x(0, z)]
    for copy in flag_x:
        copy.wait()
    ref = valid.at[pl.ds(mult(256 * c, 256), 256)]
    flag_t = remote(ref, ref, s_ft, r_ft, dev(z, x, 1 - c))
    for n, dz in ((1, 1), (2, 3), (0, 2)):
        along_z[n].wait()
        along_x.append(send_x(1 + n, (z + 4 - dz) % 4))

    def correlate_quarter(q):
        def tile(t, carry):
            all_lanes = pl.ds(mult(QUARTER * q + 128 * t, 128), 128)
            lanes = pl.ds(mult(128 * t, 128), 128)
            at = 7 * q + t
            co, si = turn[0:1, all_lanes], turn[1:2, all_lanes]
            for h in range(8):
                a = src[pl.ds(32 * h, 16), all_lanes].astype(F32)
                b = src[pl.ds(32 * h + 16, 16), all_lanes].astype(F32)
                a_turn, b_turn = a * co + b * si, b * co - a * si
                src_f[h, 0], src_f[h, 1], src_f[h, 2] = a_turn + b_turn, b_turn, a_turn
            for block in range(4):
                sums = [[None] * 3 for _ in range(4)]
                for h in range(8):
                    rec = [rec_f[at, h, k] for k in range(3)]
                    for n in range(4):
                        for k in range(3):
                            row = src_f[h, k, pl.ds(block * 4 + n, 1), :]
                            term = jnp.broadcast_to(row, (16, 128)) * rec[k]
                            sums[n][k] = term if h == 0 else sums[n][k] + term
                for n in range(4):
                    rows = pl.ds(16 * (block * 4 + n), 16)
                    cross[0, rows, lanes] = (sums[n][0] - sums[n][1]).astype(BF16)
                    cross[1, rows, lanes] = (sums[n][0] - sums[n][2]).astype(BF16)
            return carry

        lax.fori_loop(0, 7, tile, 0)
        bins = pl.ds(mult(QUARTER * q, 128), QUARTER)
        total[0] += jnp.dot(cross[0], table[bins, 0:HALF], preferred_element_type=F32)
        total[1] += jnp.dot(cross[1], table[bins, HALF:], preferred_element_type=F32)

    across = [send(half(x), s_t.at[0], r_t.at[0], dev(z, x, 1 - c))]
    flag_t.wait()
    ri = lax.broadcasted_iota(jnp.int32, (256, 512), 0)
    ci = lax.broadcasted_iota(jnp.int32, (256, 512), 1)
    target = jnp.full((256, 512), -1, jnp.int32)
    for i in range(16):
        where = 256 * (holder[i] % 2) + 64 * ((holder[i] // 2) % 4) + 16 * (holder[i] // 8) + local[i]
        target = jnp.where(ri // 16 == i, where, target)
    choose = jnp.where(ci == target, 1.0, 0.0).astype(BF16)
    shared = jnp.dot(choose, valid[...], preferred_element_type=F32) * jnp.concatenate([wide] * 16, axis=0)
    shared = jnp.sum(shared, axis=1, keepdims=True)
    scale = (1.0 / jnp.maximum(shared, 1.0)) * (1.0 / math.sqrt(BINS))

    table_copy.wait()
    across[0].wait()
    correlate_quarter(x)
    for n, dx in ((1, 1), (2, 3), (0, 2)):
        for k in range(4):
            along_x[k][n].wait()
        copy = send(half((x + 4 - dx) % 4), s_t.at[1 + n], r_t.at[1 + n], dev(z, x, 1 - c))
        copy.wait()
        correlate_quarter((x + 4 - dx) % 4)

    even, odd = total[0] * scale, total[1] * scale
    for n in range(4):
        daily[4 + n] = (even - odd)[:, 128 * n:128 * n + 128].astype(BF16)
    back = jnp.dot((even + odd).astype(BF16), mirror[...], preferred_element_type=F32)
    for n in range(4):
        daily[n] = back[:, 128 * n:128 * n + 128].astype(BF16)
    copies = []
    for n in (4, 3, 5, 2, 6, 1, 7):
        to = (day + n) % 8
        copies.append(remote(daily.at[to], days.at[n - 1], s_d.at[n - 1], r_d.at[n - 1], (to, me)))
    for copy in copies:
        copy.wait()
    result = daily[day].astype(F32)
    for n in range(7):
        result = result + days[n].astype(F32)
    out[...] = result


def fused(sources, station_rows, spectra, flags):
    table, turn, mirror = tables()
    sem = pltpu.SemaphoreType.DMA
    vmem = pl.BlockSpec(memory_space=pltpu.VMEM)
    smem = pl.BlockSpec(memory_space=pltpu.SMEM)
    return pl.pallas_call(
        fused_kernel,
        out_shape=(jax.ShapeDtypeStruct((256, 128), F32), jax.ShapeDtypeStruct((1,), jnp.int32)),
        in_specs=[smem, smem, vmem, vmem, pl.BlockSpec(memory_space=pl.ANY), vmem, vmem],
        out_specs=(vmem, smem),
        scratch_shapes=[
            pltpu.VMEM((BINS, LAGS), BF16),
            pltpu.VMEM((256, BINS), BF16),
            pltpu.VMEM((64, BINS), BF16),
            pltpu.VMEM((256, QUARTER), BF16),
            pltpu.VMEM((64, QUARTER), BF16),
            pltpu.VMEM((32, QUARTER), BF16),
            pltpu.VMEM((256, BINS), BF16),
            pltpu.VMEM((512, 128), BF16),
            pltpu.VMEM((2, 256, QUARTER), BF16),
            pltpu.VMEM((2, 256, HALF), F32),
            pltpu.VMEM((BINS // 128, 8, 3, 16, 128), F32),
            pltpu.VMEM((8, 3, 16, 128), F32),
            pltpu.VMEM((7, 256, 128), BF16),
            pltpu.VMEM((8, 256, 128), BF16),
            sem,
            sem((15,)), sem((15,)), sem, sem, sem((3,)), sem((3,)), sem((4, 3)), sem((4, 3)), sem((4,)), sem((4,)),
            sem((3,)), sem((3,)), sem((3,)), sem((3,)), sem, sem, sem((7,)), sem((7,)),
        ],
        compiler_params=pltpu.CompilerParams(collective_id=0, has_side_effects=True, vmem_limit_bytes=52 << 20),
    )(sources, station_rows, spectra, flags, jnp.asarray(table), jnp.asarray(turn), jnp.asarray(mirror))


def general(spectra, hour_flags, sources, station_rows):
    me = lax.axis_index("sta")
    values = spectra[0].astype(F32)
    power = jnp.mean(values * values, axis=(2, 3))
    valid = hour_flags[0].astype(F32)
    white = (values * (valid / jnp.sqrt(power + EPSILON))[:, :, None, None]).astype(BF16)
    white = white.reshape(16, 16, BINS).transpose(1, 0, 2)
    rows = station_rows[sources.reshape(-1)]
    holder, local = rows // 16, rows % 16
    mine = (holder == me)[:, None]
    source_valid = lax.psum(jnp.where(mine, valid[local], 0.0), "sta")
    shared = jnp.dot(source_valid, valid.T, precision=lax.Precision.HIGHEST)
    weights = (1.0 / jnp.maximum(shared, 1.0)).reshape(256, 1) * (1.0 / math.sqrt(BINS))
    kept = jnp.where(mine, white[:, local], 0).astype(BF16)
    src = lax.psum(kept.reshape(256, BINS), "sta")
    term = correlate(white.reshape(256, BINS), src, weights).astype(F32)
    return lax.psum_scatter(term, "day", scatter_dimension=1, tiled=True)


def shards(spectra, hour_flags, sources, station_rows):
    stacked, load = fused(sources, station_rows, spectra.reshape(256, BINS), hour_flags[0])
    stacked = lax.cond(
        load[0] <= SLOTS,
        lambda *args: stacked,
        general,
        spectra, hour_flags, sources, station_rows,
    )
    return stacked.reshape(16, 16, 128)


def solution(mesh):
    in_specs = (P("day", "sta", None, None, None), P("day", "sta", None), P(), P())
    out_specs = P(None, "sta", "day")
    return jax.shard_map(shards, mesh=mesh, in_specs=in_specs, out_specs=out_specs, check_vma=False)
```

```python
import functools
import math

import jax
import jax.numpy as jnp
import ml_dtypes
import numpy as np
from jax import lax
from jax.experimental import pallas as pl
from jax.experimental.pallas import tpu as pltpu
from jax.sharding import PartitionSpec as P

BINS = 3584
LAGS = 1024
HALF = LAGS // 2
QUARTER = BINS // 4
EPSILON = 1e-06
SLOTS = 4
MESH = pl.DeviceIdType.MESH
BF16 = jnp.bfloat16
F32 = jnp.float32


def tables():
    bins = np.arange(BINS, dtype=np.int64)[:, None]
    half_lags = 2 * np.arange(HALF, dtype=np.int64)[None] + 1
    angles = np.pi * ((bins * half_lags) % (4 * BINS)) / (2 * BINS)
    table = np.concatenate([np.cos(angles), np.sin(angles)], 1).astype(ml_dtypes.bfloat16)
    shift = np.pi * np.arange(BINS) / (2 * BINS)
    turn = np.stack([np.cos(shift), np.sin(shift)]).astype(np.float32)
    mirror = np.eye(HALF)[::-1].astype(ml_dtypes.bfloat16)
    return table, turn, mirror


def mult(value, k):
    return pl.multiple_of(value, k)


def correlate_kernel(white, src, table, turn, mirror, weights, out, cross, total, rec_f, src_f):
    step = pl.program_id(0)
    tiles = white.shape[1] // 128

    @pl.when(step == 0)
    def _():
        total[...] = jnp.zeros_like(total)

    for t in range(tiles):
        lanes = pl.ds(t * 128, 128)
        co, si = turn[0:1, lanes], turn[1:2, lanes]
        for h in range(8):
            c = white[pl.ds(32 * h, 16), lanes].astype(F32)
            e = white[pl.ds(32 * h + 16, 16), lanes].astype(F32)
            rec_f[t, h, 0], rec_f[t, h, 1], rec_f[t, h, 2] = c, c - e, c + e
            a = src[pl.ds(32 * h, 16), lanes].astype(F32)
            b = src[pl.ds(32 * h + 16, 16), lanes].astype(F32)
            a_turn, b_turn = a * co + b * si, b * co - a * si
            src_f[t, h, 0], src_f[t, h, 1], src_f[t, h, 2] = a_turn + b_turn, b_turn, a_turn
    for t in range(tiles):
        lanes = pl.ds(t * 128, 128)
        for block in range(4):
            sums = [[None] * 3 for _ in range(4)]
            for h in range(8):
                rec = [rec_f[t, h, k] for k in range(3)]
                for n in range(4):
                    for k in range(3):
                        row = src_f[t, h, k, pl.ds(block * 4 + n, 1), :]
                        term = jnp.broadcast_to(row, (16, 128)) * rec[k]
                        sums[n][k] = term if h == 0 else sums[n][k] + term
            for n in range(4):
                rows = pl.ds(16 * (block * 4 + n), 16)
                cross[0, rows, lanes] = (sums[n][0] - sums[n][1]).astype(BF16)
                cross[1, rows, lanes] = (sums[n][0] - sums[n][2]).astype(BF16)
    total[0] += jnp.dot(cross[0], table[:, 0:HALF], preferred_element_type=F32)
    total[1] += jnp.dot(cross[1], table[:, HALF:], preferred_element_type=F32)

    @pl.when(step == pl.num_programs(0) - 1)
    def _():
        scale = weights[...]
        even, odd = total[0] * scale, total[1] * scale
        out[:, HALF:] = (even - odd).astype(BF16)
        back = jnp.dot((even + odd).astype(BF16), mirror[...], preferred_element_type=F32)
        out[:, 0:HALF] = back.astype(BF16)


def correlate(white, src, weights):
    table, turn, mirror = tables()
    width = QUARTER
    return pl.pallas_call(
        correlate_kernel,
        grid=(BINS // width,),
        out_shape=jax.ShapeDtypeStruct((256, LAGS), BF16),
        in_specs=[
            pl.BlockSpec((256, width), lambda q: (0, q)),
            pl.BlockSpec((256, width), lambda q: (0, q)),
            pl.BlockSpec((width, LAGS), lambda q: (q, 0)),
            pl.BlockSpec((2, width), lambda q: (0, q)),
            pl.BlockSpec((HALF, HALF), lambda q: (0, 0)),
            pl.BlockSpec((256, 1), lambda q: (0, 0)),
        ],
        out_specs=pl.BlockSpec((256, LAGS), lambda q: (0, 0)),
        scratch_shapes=[
            pltpu.VMEM((2, 256, width), BF16),
            pltpu.VMEM((2, 256, HALF), F32),
            pltpu.VMEM((width // 128, 8, 3, 16, 128), F32),
            pltpu.VMEM((width // 128, 8, 3, 16, 128), F32),
        ],
        compiler_params=pltpu.CompilerParams(vmem_limit_bytes=48 << 20),
    )(white, src, jnp.asarray(table), jnp.asarray(turn), jnp.asarray(mirror), weights)


def fused_kernel(sources, rows_ref, spectra_hbm, flags, table_hbm, turn, mirror, out, load, spectra, table, white, slots, recv, picked,
                 twin, src, valid, cross, total, rec_f, src_f, days, daily, s_spec, s_tab, s_sc, r_sc, s_tw, r_tw, s_z, r_z,
                 s_x, r_x, s_t, r_t, s_fz, r_fz, s_fx, r_fx, s_ft, r_ft, s_d, r_d):
    day = lax.axis_index("day")
    me = lax.axis_index("sta")
    z, x, c, chip = me // 8, (me // 2) % 4, me % 2, me // 2

    def dev(z_to, x_to, c_to):
        return (day, z_to * 8 + x_to * 2 + c_to)

    def remote(source, target, s_sem, r_sem, device):
        copy = pltpu.make_async_remote_copy(
            src_ref=source, dst_ref=target, send_sem=s_sem, recv_sem=r_sem, device_id=device, device_id_type=MESH
        )
        copy.start()
        return copy

    spectra_copy = pltpu.make_async_copy(spectra_hbm, spectra, s_spec)
    spectra_copy.start()
    offsets = [(dz, dx) for dz in (2, 1, 3, 0) for dx in (2, 1, 3, 0) if (dz, dx) != (0, 0)]
    barrier = pltpu.get_barrier_semaphore()
    for dz, dx in offsets:
        pl.semaphore_signal(barrier, inc=1, device_id=dev((z + dz) % 4, (x + dx) % 4, c), device_id_type=MESH)
    pl.semaphore_signal(barrier, inc=1, device_id=dev(z, x, 1 - c), device_id_type=MESH)
    for n in range(1, 8):
        pl.semaphore_signal(barrier, inc=1, device_id=((day + n) % 8, me), device_id_type=MESH)
    table_copy = pltpu.make_async_copy(table_hbm, table, s_tab)
    table_copy.start()

    ri = lax.broadcasted_iota(jnp.int32, (256, 256), 0)
    ci = lax.broadcasted_iota(jnp.int32, (256, 256), 1)
    natural = (ri % 16) * 16 + 4 * ((ri // 32) % 4) + 2 * (ri // 128) + (ri // 16) % 2
    order = jnp.where(ci == natural, 1.0, 0.0).astype(BF16)
    power = jnp.zeros((256, 128), F32)
    spectra_copy.wait()
    for k in range(BINS // 256):
        lanes = pl.ds(256 * k, 256)
        values = jnp.dot(order, spectra[:, :, :, lanes].reshape(256, 256), preferred_element_type=F32)
        white[:, lanes] = values.astype(BF16)
        squares = values * values
        power = power + squares[:, :128] + squares[:, 128:]
    power = jnp.sum(power, axis=1, keepdims=True)
    flag = flags[...].astype(F32)
    for h in range(8):
        hour = 2 * (h % 4) + h // 4
        mean = (power[32 * h:32 * h + 16] + power[32 * h + 16:32 * h + 32]) * (1.0 / (2 * BINS))
        scale = flag[:, hour:hour + 1] / jnp.sqrt(mean + EPSILON)
        for p in range(2):
            rows = pl.ds(32 * h + 16 * p, 16)
            white[rows, :] = (white[rows, :].astype(F32) * scale).astype(BF16)
    wide = jnp.concatenate([flag, jnp.zeros((16, 120), F32)], axis=1)
    own_flags = pl.ds(mult(256 * c + 64 * x + 16 * z, 16), 16)
    valid[own_flags, :] = wide.astype(BF16)

    holder, local, rank = [], [], []
    most = jnp.int32(0)
    for i in range(16):
        row = rows_ref[sources[i // 8, i % 8]]
        holder.append(row // 16)
        local.append(row % 16)
        count = jnp.int32(0)
        for j in range(i):
            count = count + jnp.where(holder[j] == holder[i], 1, 0)
        rank.append(count)
        most = jnp.maximum(most, count + 1)
    load[0] = most
    ri, ci = ri[:64], ci[:64]
    target = jnp.full((64, 256), -1, jnp.int32)
    base = 128 * ((ri // 8) % 2) + 32 * (ri // 16) + 16 * ((ri // 4) % 2)
    for i in range(16):
        key = jnp.where(holder[i] == me, rank[i], 99)
        target = jnp.where(ri % 4 == key, base + local[i], target)
    pick = jnp.where(ci == target, 1.0, 0.0).astype(BF16)
    slots[...] = jnp.dot(pick, white[...], preferred_element_type=F32).astype(BF16)
    pl.semaphore_wait(barrier, 23)

    copies = []
    for n, (dz, dx) in enumerate(offsets):
        z_to, x_to = (z + dz) % 4, (x + dx) % 4
        copies.append(
            remote(
                slots.at[pl.ds(mult(16 * z_to, 16), 16), pl.ds(mult(QUARTER * x_to, 128), QUARTER)],
                recv.at[pl.ds(mult(16 * chip, 16), 16)],
                s_sc.at[n],
                r_sc.at[n],
                dev(z_to, x_to, c),
            )
        )
    ref = valid.at[own_flags]
    flag_z = [remote(ref, ref, s_fz.at[n], r_fz.at[n], dev((z + 1 + n) % 4, x, c)) for n in range(3)]
    recv[pl.ds(mult(16 * chip, 16), 16), :] = slots[
        pl.ds(mult(16 * z, 16), 16), pl.ds(mult(QUARTER * x, 128), QUARTER)
    ]
    target = jnp.full((64, 256), -1, jnp.int32)
    for i in range(16):
        where = jnp.where(holder[i] % 2 == c, 16 * (holder[i] // 2) + rank[i], -1000)
        target = jnp.where(ri % 16 == i, where + 8 * (ri // 32) + 4 * ((ri // 16) % 2), target)
    pick = jnp.where(ci == target, 1.0, 0.0).astype(BF16)

    def receiver_planes(t, carry):
        lanes = pl.ds(mult(t * 128, 128), 128)
        for h in range(8):
            cosine = white[pl.ds(32 * h, 16), lanes].astype(F32)
            sine = white[pl.ds(32 * h + 16, 16), lanes].astype(F32)
            rec_f[t, h, 0] = cosine
            rec_f[t, h, 1] = cosine - sine
            rec_f[t, h, 2] = cosine + sine
        return carry

    lax.fori_loop(0, BINS // 128, receiver_planes, 0)
    total[...] = jnp.zeros_like(total)

    for copy in flag_z:
        copy.wait()
    ref = valid.at[pl.ds(mult(256 * c + 64 * x, 64), 64)]
    flag_x = [remote(ref, ref, s_fx.at[n], r_fx.at[n], dev(z, (x + 1 + n) % 4, c)) for n in range(3)]
    for copy in copies:
        copy.wait()
    picked[...] = jnp.dot(pick, recv[...], preferred_element_type=F32).astype(BF16)
    copy = remote(picked.at[pl.ds(mult(32 * (1 - c), 32), 32)], twin, s_tw, r_tw, dev(z, x, 1 - c))
    copy.wait()

    def piece(z_of, x_of):
        return src.at[pl.ds(mult(128 * c + 32 * z_of, 32), 32), pl.ds(mult(QUARTER * x_of, 128), QUARTER)]

    def half(x_of):
        return src.at[pl.ds(mult(128 * c, 128), 128), pl.ds(mult(QUARTER * x_of, 128), QUARTER)]

    def send(ref, s_sem, r_sem, device):
        return remote(ref, ref, s_sem, r_sem, device)

    piece(z, x)[...] = picked[pl.ds(mult(32 * c, 32), 32), :] + twin[...]

    def send_x(k, z_of):
        return [
            send(piece(z_of, x), s_x.at[k, n], r_x.at[k, n], dev(z, (x + dx) % 4, c))
            for n, dx in enumerate((2, 1, 3))
        ]

    along_z = [send(piece(z, x), s_z.at[n], r_z.at[n], dev((z + dz) % 4, x, c)) for n, dz in enumerate((2, 1, 3))]
    along_x = [send_x(0, z)]
    for copy in flag_x:
        copy.wait()
    ref = valid.at[pl.ds(mult(256 * c, 256), 256)]
    flag_t = remote(ref, ref, s_ft, r_ft, dev(z, x, 1 - c))
    for n, dz in ((1, 1), (2, 3), (0, 2)):
        along_z[n].wait()
        along_x.append(send_x(1 + n, (z + 4 - dz) % 4))

    def correlate_quarter(q):
        def tile(t, carry):
            all_lanes = pl.ds(mult(QUARTER * q + 128 * t, 128), 128)
            lanes = pl.ds(mult(128 * t, 128), 128)
            at = 7 * q + t
            co, si = turn[0:1, all_lanes], turn[1:2, all_lanes]
            for h in range(8):
                a = src[pl.ds(32 * h, 16), all_lanes].astype(F32)
                b = src[pl.ds(32 * h + 16, 16), all_lanes].astype(F32)
                a_turn, b_turn = a * co + b * si, b * co - a * si
                src_f[h, 0], src_f[h, 1], src_f[h, 2] = a_turn + b_turn, b_turn, a_turn
            for block in range(4):
                sums = [[None] * 3 for _ in range(4)]
                for h in range(8):
                    rec = [rec_f[at, h, k] for k in range(3)]
                    for n in range(4):
                        for k in range(3):
                            row = src_f[h, k, pl.ds(block * 4 + n, 1), :]
                            term = jnp.broadcast_to(row, (16, 128)) * rec[k]
                            sums[n][k] = term if h == 0 else sums[n][k] + term
                for n in range(4):
                    rows = pl.ds(16 * (block * 4 + n), 16)
                    cross[0, rows, lanes] = (sums[n][0] - sums[n][1]).astype(BF16)
                    cross[1, rows, lanes] = (sums[n][0] - sums[n][2]).astype(BF16)
            return carry

        lax.fori_loop(0, 7, tile, 0)
        bins = pl.ds(mult(QUARTER * q, 128), QUARTER)
        total[0] += jnp.dot(cross[0], table[bins, 0:HALF], preferred_element_type=F32)
        total[1] += jnp.dot(cross[1], table[bins, HALF:], preferred_element_type=F32)

    across = [send(half(x), s_t.at[0], r_t.at[0], dev(z, x, 1 - c))]
    flag_t.wait()
    ri = lax.broadcasted_iota(jnp.int32, (256, 512), 0)
    ci = lax.broadcasted_iota(jnp.int32, (256, 512), 1)
    target = jnp.full((256, 512), -1, jnp.int32)
    for i in range(16):
        where = 256 * (holder[i] % 2) + 64 * ((holder[i] // 2) % 4) + 16 * (holder[i] // 8) + local[i]
        target = jnp.where(ri // 16 == i, where, target)
    choose = jnp.where(ci == target, 1.0, 0.0).astype(BF16)
    shared = jnp.dot(choose, valid[...], preferred_element_type=F32) * jnp.concatenate([wide] * 16, axis=0)
    shared = jnp.sum(shared, axis=1, keepdims=True)
    scale = (1.0 / jnp.maximum(shared, 1.0)) * (1.0 / math.sqrt(BINS))

    table_copy.wait()
    across[0].wait()
    correlate_quarter(x)
    for n, dx in ((1, 1), (2, 3), (0, 2)):
        for k in range(4):
            along_x[k][n].wait()
        copy = send(half((x + 4 - dx) % 4), s_t.at[1 + n], r_t.at[1 + n], dev(z, x, 1 - c))
        copy.wait()
        correlate_quarter((x + 4 - dx) % 4)

    even, odd = total[0] * scale, total[1] * scale
    for n in range(4):
        daily[4 + n] = (even - odd)[:, 128 * n:128 * n + 128].astype(BF16)
    back = jnp.dot((even + odd).astype(BF16), mirror[...], preferred_element_type=F32)
    for n in range(4):
        daily[n] = back[:, 128 * n:128 * n + 128].astype(BF16)
    copies = []
    for n in (4, 3, 5, 2, 6, 1, 7):
        to = (day + n) % 8
        copies.append(remote(daily.at[to], days.at[n - 1], s_d.at[n - 1], r_d.at[n - 1], (to, me)))
    for copy in copies:
        copy.wait()
    result = daily[day].astype(F32)
    for n in range(7):
        result = result + days[n].astype(F32)
    out[...] = result


def fused(sources, station_rows, spectra, flags):
    table, turn, mirror = tables()
    sem = pltpu.SemaphoreType.DMA
    vmem = pl.BlockSpec(memory_space=pltpu.VMEM)
    smem = pl.BlockSpec(memory_space=pltpu.SMEM)
    hbm = pl.BlockSpec(memory_space=pl.ANY)
    return pl.pallas_call(
        fused_kernel,
        out_shape=(jax.ShapeDtypeStruct((256, 128), F32), jax.ShapeDtypeStruct((1,), jnp.int32)),
        in_specs=[smem, smem, hbm, vmem, hbm, vmem, vmem],
        out_specs=(vmem, smem),
        scratch_shapes=[
            pltpu.VMEM((16, 8, 2, BINS), BF16),
            pltpu.VMEM((BINS, LAGS), BF16),
            pltpu.VMEM((256, BINS), BF16),
            pltpu.VMEM((64, BINS), BF16),
            pltpu.VMEM((256, QUARTER), BF16),
            pltpu.VMEM((64, QUARTER), BF16),
            pltpu.VMEM((32, QUARTER), BF16),
            pltpu.VMEM((256, BINS), BF16),
            pltpu.VMEM((512, 128), BF16),
            pltpu.VMEM((2, 256, QUARTER), BF16),
            pltpu.VMEM((2, 256, HALF), F32),
            pltpu.VMEM((BINS // 128, 8, 3, 16, 128), F32),
            pltpu.VMEM((8, 3, 16, 128), F32),
            pltpu.VMEM((7, 256, 128), BF16),
            pltpu.VMEM((8, 256, 128), BF16),
            sem, sem,
            sem((15,)), sem((15,)), sem, sem, sem((3,)), sem((3,)), sem((4, 3)), sem((4, 3)), sem((4,)), sem((4,)),
            sem((3,)), sem((3,)), sem((3,)), sem((3,)), sem, sem, sem((7,)), sem((7,)),
        ],
        compiler_params=pltpu.CompilerParams(collective_id=0, has_side_effects=True, vmem_limit_bytes=52 << 20),
    )(sources, station_rows, spectra, flags, jnp.asarray(table), jnp.asarray(turn), jnp.asarray(mirror))


def sum_over(value, axis, size):
    step = 1
    while step < size:
        value = value + lax.ppermute(value, axis, [(n, n ^ step) for n in range(size)])
        step *= 2
    return value


def general(spectra, hour_flags, sources, station_rows):
    me = lax.axis_index("sta")
    values = spectra[0].astype(F32)
    power = jnp.mean(values * values, axis=(2, 3))
    valid = hour_flags[0].astype(F32)
    white = (values * (valid / jnp.sqrt(power + EPSILON))[:, :, None, None]).astype(BF16)
    white = white.reshape(16, 16, BINS).transpose(1, 0, 2)
    rows = station_rows[sources.reshape(-1)]
    holder, local = rows // 16, rows % 16
    mine = (holder == me)[:, None]
    source_valid = sum_over(jnp.where(mine, valid[local], 0.0), "sta", 32)
    shared = jnp.dot(source_valid, valid.T, precision=lax.Precision.HIGHEST)
    weights = (1.0 / jnp.maximum(shared, 1.0)).reshape(256, 1) * (1.0 / math.sqrt(BINS))
    kept = jnp.where(mine, white[:, local], 0).astype(BF16)
    src = sum_over(kept.reshape(256, BINS), "sta", 32)
    term = correlate(white.reshape(256, BINS), src, weights).astype(F32)
    term = sum_over(term, "day", 8)
    return lax.dynamic_slice_in_dim(term, 128 * lax.axis_index("day"), 128, 1)


def shards(spectra, hour_flags, sources, station_rows):
    stacked, load = fused(sources, station_rows, spectra[0], hour_flags[0])
    stacked = lax.cond(
        load[0] <= SLOTS,
        lambda *args: stacked,
        general,
        spectra, hour_flags, sources, station_rows,
    )
    return stacked.reshape(16, 16, 128)


def solution(mesh):
    in_specs = (P("day", "sta", None, None, None), P("day", "sta", None), P(), P())
    out_specs = P(None, "sta", "day")
    return jax.shard_map(shards, mesh=mesh, in_specs=in_specs, out_specs=out_specs, check_vma=False)
```

```python
import functools
import math

import jax
import jax.numpy as jnp
import ml_dtypes
import numpy as np
from jax import lax
from jax.experimental import pallas as pl
from jax.experimental.pallas import tpu as pltpu
from jax.sharding import PartitionSpec as P

BINS = 3584
LAGS = 1024
HALF = LAGS // 2
QUARTER = BINS // 4
EPSILON = 1e-06
SLOTS = 4
PARTS = ((0, 512), (512, 384))
MESH = pl.DeviceIdType.MESH
BF16 = jnp.bfloat16
F32 = jnp.float32


def tables():
    bins = np.arange(BINS, dtype=np.int64)[:, None]
    half_lags = 2 * np.arange(HALF, dtype=np.int64)[None] + 1
    angles = np.pi * ((bins * half_lags) % (4 * BINS)) / (2 * BINS)
    table = np.concatenate([np.cos(angles), np.sin(angles)], 1).astype(ml_dtypes.bfloat16)
    shift = np.pi * np.arange(BINS) / (2 * BINS)
    turn = np.stack([np.cos(shift), np.sin(shift)]).astype(np.float32)
    mirror = np.eye(HALF)[::-1].astype(ml_dtypes.bfloat16)
    return table, turn, mirror


def mult(value, k):
    return pl.multiple_of(value, k)


def correlate_kernel(white, src, table, turn, mirror, weights, out, cross, total, rec_f, src_f):
    step = pl.program_id(0)
    tiles = white.shape[1] // 128

    @pl.when(step == 0)
    def _():
        total[...] = jnp.zeros_like(total)

    for t in range(tiles):
        lanes = pl.ds(t * 128, 128)
        co, si = turn[0:1, lanes], turn[1:2, lanes]
        for h in range(8):
            c = white[pl.ds(32 * h, 16), lanes].astype(F32)
            e = white[pl.ds(32 * h + 16, 16), lanes].astype(F32)
            rec_f[t, h, 0], rec_f[t, h, 1], rec_f[t, h, 2] = c, c - e, c + e
            a = src[pl.ds(32 * h, 16), lanes].astype(F32)
            b = src[pl.ds(32 * h + 16, 16), lanes].astype(F32)
            a_turn, b_turn = a * co + b * si, b * co - a * si
            src_f[t, h, 0], src_f[t, h, 1], src_f[t, h, 2] = a_turn + b_turn, b_turn, a_turn
    for t in range(tiles):
        lanes = pl.ds(t * 128, 128)
        for block in range(4):
            sums = [[None] * 3 for _ in range(4)]
            for h in range(8):
                rec = [rec_f[t, h, k] for k in range(3)]
                for n in range(4):
                    for k in range(3):
                        row = src_f[t, h, k, pl.ds(block * 4 + n, 1), :]
                        term = jnp.broadcast_to(row, (16, 128)) * rec[k]
                        sums[n][k] = term if h == 0 else sums[n][k] + term
            for n in range(4):
                rows = pl.ds(16 * (block * 4 + n), 16)
                cross[0, rows, lanes] = (sums[n][0] - sums[n][1]).astype(BF16)
                cross[1, rows, lanes] = (sums[n][0] - sums[n][2]).astype(BF16)
    total[0] += jnp.dot(cross[0], table[:, 0:HALF], preferred_element_type=F32)
    total[1] += jnp.dot(cross[1], table[:, HALF:], preferred_element_type=F32)

    @pl.when(step == pl.num_programs(0) - 1)
    def _():
        scale = weights[...]
        even, odd = total[0] * scale, total[1] * scale
        out[:, HALF:] = (even - odd).astype(BF16)
        back = jnp.dot((even + odd).astype(BF16), mirror[...], preferred_element_type=F32)
        out[:, 0:HALF] = back.astype(BF16)


def correlate(white, src, weights):
    table, turn, mirror = tables()
    width = QUARTER
    return pl.pallas_call(
        correlate_kernel,
        grid=(BINS // width,),
        out_shape=jax.ShapeDtypeStruct((256, LAGS), BF16),
        in_specs=[
            pl.BlockSpec((256, width), lambda q: (0, q)),
            pl.BlockSpec((256, width), lambda q: (0, q)),
            pl.BlockSpec((width, LAGS), lambda q: (q, 0)),
            pl.BlockSpec((2, width), lambda q: (0, q)),
            pl.BlockSpec((HALF, HALF), lambda q: (0, 0)),
            pl.BlockSpec((256, 1), lambda q: (0, 0)),
        ],
        out_specs=pl.BlockSpec((256, LAGS), lambda q: (0, 0)),
        scratch_shapes=[
            pltpu.VMEM((2, 256, width), BF16),
            pltpu.VMEM((2, 256, HALF), F32),
            pltpu.VMEM((width // 128, 8, 3, 16, 128), F32),
            pltpu.VMEM((width // 128, 8, 3, 16, 128), F32),
        ],
        compiler_params=pltpu.CompilerParams(vmem_limit_bytes=48 << 20),
    )(white, src, jnp.asarray(table), jnp.asarray(turn), jnp.asarray(mirror), weights)


def fused_kernel(sources, rows_ref, spectra_hbm, flags, table_hbm, turn, mirror, out, load, spectra, table, white, slots, recv, picked,
                 twin, src, valid, cross, total, rec_f, src_f, days, daily, s_spec, s_tab, s_sc, r_sc, s_tw, r_tw, s_z, r_z,
                 s_x, r_x, s_t, r_t, s_fz, r_fz, s_fx, r_fx, s_ft, r_ft, s_d, r_d):
    day = lax.axis_index("day")
    me = lax.axis_index("sta")
    z, x, c, chip = me // 8, (me // 2) % 4, me % 2, me // 2

    def dev(z_to, x_to, c_to):
        return (day, z_to * 8 + x_to * 2 + c_to)

    def remote(source, target, s_sem, r_sem, device):
        copy = pltpu.make_async_remote_copy(
            src_ref=source, dst_ref=target, send_sem=s_sem, recv_sem=r_sem, device_id=device, device_id_type=MESH
        )
        copy.start()
        return copy

    spectra_copy = pltpu.make_async_copy(spectra_hbm, spectra, s_spec)
    spectra_copy.start()
    offsets = [(dz, dx) for dz in (2, 1, 3, 0) for dx in (2, 1, 3, 0) if (dz, dx) != (0, 0)]
    barrier = pltpu.get_barrier_semaphore()
    for dz, dx in offsets:
        pl.semaphore_signal(barrier, inc=1, device_id=dev((z + dz) % 4, (x + dx) % 4, c), device_id_type=MESH)
    pl.semaphore_signal(barrier, inc=1, device_id=dev(z, x, 1 - c), device_id_type=MESH)
    for n in range(1, 8):
        pl.semaphore_signal(barrier, inc=1, device_id=((day + n) % 8, me), device_id_type=MESH)
    table_copy = pltpu.make_async_copy(table_hbm, table, s_tab)
    table_copy.start()

    ri = lax.broadcasted_iota(jnp.int32, (256, 256), 0)
    ci = lax.broadcasted_iota(jnp.int32, (256, 256), 1)
    natural = (ri % 16) * 16 + 4 * ((ri // 32) % 4) + 2 * (ri // 128) + (ri // 16) % 2
    order = jnp.where(ci == natural, 1.0, 0.0).astype(BF16)
    power = jnp.zeros((256, 128), F32)
    spectra_copy.wait()
    for k in range(BINS // 256):
        lanes = pl.ds(256 * k, 256)
        values = jnp.dot(order, spectra[:, :, :, lanes].reshape(256, 256), preferred_element_type=F32)
        white[:, lanes] = values.astype(BF16)
        squares = values * values
        power = power + squares[:, :128] + squares[:, 128:]
    power = jnp.sum(power, axis=1, keepdims=True)
    flag = flags[0].astype(F32)
    for h in range(8):
        hour = 2 * (h % 4) + h // 4
        mean = (power[32 * h:32 * h + 16] + power[32 * h + 16:32 * h + 32]) * (1.0 / (2 * BINS))
        scale = flag[:, hour:hour + 1] / jnp.sqrt(mean + EPSILON)
        for p in range(2):
            rows = pl.ds(32 * h + 16 * p, 16)
            white[rows, :] = (white[rows, :].astype(F32) * scale).astype(BF16)
    wide = jnp.concatenate([flag, jnp.zeros((16, 120), F32)], axis=1)
    own_flags = pl.ds(mult(256 * c + 64 * x + 16 * z, 16), 16)
    valid[own_flags, :] = wide.astype(BF16)

    holder, local, rank = [], [], []
    most = jnp.int32(0)
    for i in range(16):
        row = rows_ref[sources[i // 8, i % 8]]
        holder.append(row // 16)
        local.append(row % 16)
        count = jnp.int32(0)
        for j in range(i):
            count = count + jnp.where(holder[j] == holder[i], 1, 0)
        rank.append(count)
        most = jnp.maximum(most, count + 1)
    load[0] = most
    ri, ci = ri[:64], ci[:64]
    target = jnp.full((64, 256), -1, jnp.int32)
    base = 128 * ((ri // 8) % 2) + 32 * (ri // 16) + 16 * ((ri // 4) % 2)
    for i in range(16):
        key = jnp.where(holder[i] == me, rank[i], 99)
        target = jnp.where(ri % 4 == key, base + local[i], target)
    pick = jnp.where(ci == target, 1.0, 0.0).astype(BF16)
    slots[...] = jnp.dot(pick, white[...], preferred_element_type=F32).astype(BF16)
    pl.semaphore_wait(barrier, 23)

    def lanes_of(x_of, part):
        start, width = PARTS[part]
        return pl.ds(mult(QUARTER * x_of + start, 128), width)

    scattered = []
    for part, (start, width) in enumerate(PARTS):
        copies = []
        for n, (dz, dx) in enumerate(offsets):
            z_to, x_to = (z + dz) % 4, (x + dx) % 4
            copies.append(
                remote(
                    slots.at[pl.ds(mult(16 * z_to, 16), 16), lanes_of(x_to, part)],
                    recv.at[pl.ds(mult(16 * chip, 16), 16), pl.ds(start, width)],
                    s_sc.at[part, n],
                    r_sc.at[part, n],
                    dev(z_to, x_to, c),
                )
            )
        scattered.append(copies)
    ref = valid.at[own_flags]
    flag_z = [remote(ref, ref, s_fz.at[n], r_fz.at[n], dev((z + 1 + n) % 4, x, c)) for n in range(3)]
    recv[pl.ds(mult(16 * chip, 16), 16), :] = slots[
        pl.ds(mult(16 * z, 16), 16), pl.ds(mult(QUARTER * x, 128), QUARTER)
    ]
    target = jnp.full((64, 256), -1, jnp.int32)
    for i in range(16):
        where = jnp.where(holder[i] % 2 == c, 16 * (holder[i] // 2) + rank[i], -1000)
        target = jnp.where(ri % 16 == i, where + 8 * (ri // 32) + 4 * ((ri // 16) % 2), target)
    pick = jnp.where(ci == target, 1.0, 0.0).astype(BF16)

    def receiver_planes(t, carry):
        lanes = pl.ds(mult(t * 128, 128), 128)
        for h in range(8):
            cosine = white[pl.ds(32 * h, 16), lanes].astype(F32)
            sine = white[pl.ds(32 * h + 16, 16), lanes].astype(F32)
            rec_f[t, h, 0] = cosine
            rec_f[t, h, 1] = cosine - sine
            rec_f[t, h, 2] = cosine + sine
        return carry

    lax.fori_loop(0, BINS // 128, receiver_planes, 0)
    total[...] = jnp.zeros_like(total)

    def piece(z_of, x_of, part):
        return src.at[pl.ds(mult(128 * c + 32 * z_of, 32), 32), lanes_of(x_of, part)]

    def send(ref, s_sem, r_sem, device):
        return remote(ref, ref, s_sem, r_sem, device)

    def send_x(part, k, z_of):
        ref = piece(z_of, x, part)
        return [
            send(ref, s_x.at[part, k, n], r_x.at[part, k, n], dev(z, (x + dx) % 4, c))
            for n, dx in enumerate((2, 1, 3))
        ]

    def send_across(part, n, x_of):
        ref = src.at[pl.ds(mult(128 * c, 128), 128), lanes_of(x_of, part)]
        return send(ref, s_t.at[part, n], r_t.at[part, n], dev(z, x, 1 - c))

    along_z, along_x, across = [], [], []
    for part, (start, width) in enumerate(PARTS):
        for copy in scattered[part]:
            copy.wait()
        here = pl.ds(start, width)
        picked[:, here] = jnp.dot(pick, recv[:, here], preferred_element_type=F32).astype(BF16)
        copy = remote(
            picked.at[pl.ds(mult(32 * (1 - c), 32), 32), here],
            twin.at[:, here],
            s_tw.at[part],
            r_tw.at[part],
            dev(z, x, 1 - c),
        )
        if part == 0:
            for other in flag_z:
                other.wait()
            ref = valid.at[pl.ds(mult(256 * c + 64 * x, 64), 64)]
            flag_x = [remote(ref, ref, s_fx.at[n], r_fx.at[n], dev(z, (x + 1 + n) % 4, c)) for n in range(3)]
        copy.wait()
        ref = piece(z, x, part)
        ref[...] = picked[pl.ds(mult(32 * c, 32), 32), here] + twin[:, here]
        along_z.append(
            [
                send(ref, s_z.at[part, n], r_z.at[part, n], dev((z + dz) % 4, x, c))
                for n, dz in enumerate((2, 1, 3))
            ]
        )
        along_x.append([send_x(part, 0, z)])
    for part in range(len(PARTS)):
        for n, dz in ((1, 1), (2, 3), (0, 2)):
            along_z[part][n].wait()
            along_x[part].append(send_x(part, 1 + n, (z + 4 - dz) % 4))
        across.append([send_across(part, 0, x)])
    for copy in flag_x:
        copy.wait()
    ref = valid.at[pl.ds(mult(256 * c, 256), 256)]
    flag_t = remote(ref, ref, s_ft, r_ft, dev(z, x, 1 - c))

    def correlate_part(q, part):
        start, width = PARTS[part]

        def tile(t, carry):
            all_lanes = pl.ds(mult(QUARTER * q + start + 128 * t, 128), 128)
            lanes = pl.ds(mult(128 * t, 128), 128)
            at = 7 * q + start // 128 + t
            co, si = turn[0:1, all_lanes], turn[1:2, all_lanes]
            for h in range(8):
                a = src[pl.ds(32 * h, 16), all_lanes].astype(F32)
                b = src[pl.ds(32 * h + 16, 16), all_lanes].astype(F32)
                a_turn, b_turn = a * co + b * si, b * co - a * si
                src_f[h, 0], src_f[h, 1], src_f[h, 2] = a_turn + b_turn, b_turn, a_turn
            for block in range(4):
                sums = [[None] * 3 for _ in range(4)]
                for h in range(8):
                    rec = [rec_f[at, h, k] for k in range(3)]
                    for n in range(4):
                        for k in range(3):
                            row = src_f[h, k, pl.ds(block * 4 + n, 1), :]
                            term = jnp.broadcast_to(row, (16, 128)) * rec[k]
                            sums[n][k] = term if h == 0 else sums[n][k] + term
                for n in range(4):
                    rows = pl.ds(16 * (block * 4 + n), 16)
                    cross[0, rows, lanes] = (sums[n][0] - sums[n][1]).astype(BF16)
                    cross[1, rows, lanes] = (sums[n][0] - sums[n][2]).astype(BF16)
            return carry

        lax.fori_loop(0, width // 128, tile, 0)
        bins = lanes_of(q, part)
        total[0] += jnp.dot(cross[0, :, 0:width], table[bins, 0:HALF], preferred_element_type=F32)
        total[1] += jnp.dot(cross[1, :, 0:width], table[bins, HALF:], preferred_element_type=F32)

    def take_x(part, n, dx):
        for k in range(4):
            along_x[part][k][n].wait()
        across[part].append(send_across(part, 1 + n, (x + 4 - dx) % 4))

    table_copy.wait()
    across[0][0].wait()
    correlate_part(x, 0)
    for n, dx in ((1, 1), (2, 3)):
        take_x(0, n, dx)
    across[1][0].wait()
    correlate_part(x, 1)
    take_x(0, 0, 2)
    flag_t.wait()
    ri = lax.broadcasted_iota(jnp.int32, (256, 512), 0)
    ci = lax.broadcasted_iota(jnp.int32, (256, 512), 1)
    target = jnp.full((256, 512), -1, jnp.int32)
    for i in range(16):
        where = 256 * (holder[i] % 2) + 64 * ((holder[i] // 2) % 4) + 16 * (holder[i] // 8) + local[i]
        target = jnp.where(ri // 16 == i, where, target)
    choose = jnp.where(ci == target, 1.0, 0.0).astype(BF16)
    shared = jnp.dot(choose, valid[...], preferred_element_type=F32) * jnp.concatenate([wide] * 16, axis=0)
    shared = jnp.sum(shared, axis=1, keepdims=True)
    scale = (1.0 / jnp.maximum(shared, 1.0)) * (1.0 / math.sqrt(BINS))

    across[0][1].wait()
    correlate_part((x + 3) % 4, 0)
    for n, dx in ((1, 1), (2, 3)):
        take_x(1, n, dx)
    across[0][2].wait()
    correlate_part((x + 1) % 4, 0)
    take_x(1, 0, 2)
    across[0][3].wait()
    correlate_part((x + 2) % 4, 0)
    across[1][1].wait()
    correlate_part((x + 3) % 4, 1)
    across[1][2].wait()
    correlate_part((x + 1) % 4, 1)
    across[1][3].wait()
    correlate_part((x + 2) % 4, 1)

    even, odd = total[0] * scale, total[1] * scale
    for n in range(4):
        daily[4 + n] = (even - odd)[:, 128 * n:128 * n + 128].astype(BF16)
    back = jnp.dot((even + odd).astype(BF16), mirror[...], preferred_element_type=F32)
    for n in range(4):
        daily[n] = back[:, 128 * n:128 * n + 128].astype(BF16)
    copies = []
    for n in (4, 3, 5, 2, 6, 1, 7):
        to = (day + n) % 8
        copies.append(remote(daily.at[to], days.at[n - 1], s_d.at[n - 1], r_d.at[n - 1], (to, me)))
    for copy in copies:
        copy.wait()
    result = daily[day].astype(F32)
    for n in range(7):
        result = result + days[n].astype(F32)
    out[...] = result


def fused(sources, station_rows, spectra, flags):
    table, turn, mirror = tables()
    sem = pltpu.SemaphoreType.DMA
    vmem = pl.BlockSpec(memory_space=pltpu.VMEM)
    smem = pl.BlockSpec(memory_space=pltpu.SMEM)
    hbm = pl.BlockSpec(memory_space=pl.ANY)
    return pl.pallas_call(
        fused_kernel,
        out_shape=(jax.ShapeDtypeStruct((256, 128), F32), jax.ShapeDtypeStruct((1,), jnp.int32)),
        in_specs=[smem, smem, hbm, vmem, hbm, vmem, vmem],
        out_specs=(vmem, smem),
        scratch_shapes=[
            pltpu.VMEM((16, 8, 2, BINS), BF16),
            pltpu.VMEM((BINS, LAGS), BF16),
            pltpu.VMEM((256, BINS), BF16),
            pltpu.VMEM((64, BINS), BF16),
            pltpu.VMEM((256, QUARTER), BF16),
            pltpu.VMEM((64, QUARTER), BF16),
            pltpu.VMEM((32, QUARTER), BF16),
            pltpu.VMEM((256, BINS), BF16),
            pltpu.VMEM((512, 128), BF16),
            pltpu.VMEM((2, 256, QUARTER), BF16),
            pltpu.VMEM((2, 256, HALF), F32),
            pltpu.VMEM((BINS // 128, 8, 3, 16, 128), F32),
            pltpu.VMEM((8, 3, 16, 128), F32),
            pltpu.VMEM((7, 256, 128), BF16),
            pltpu.VMEM((8, 256, 128), BF16),
            sem, sem,
            sem((2, 15)), sem((2, 15)), sem((2,)), sem((2,)), sem((2, 3)), sem((2, 3)), sem((2, 4, 3)), sem((2, 4, 3)),
            sem((2, 4)), sem((2, 4)),
            sem((3,)), sem((3,)), sem((3,)), sem((3,)), sem, sem, sem((7,)), sem((7,)),
        ],
        compiler_params=pltpu.CompilerParams(collective_id=0, has_side_effects=True, vmem_limit_bytes=52 << 20),
    )(sources, station_rows, spectra, flags, jnp.asarray(table), jnp.asarray(turn), jnp.asarray(mirror))


def sum_over(value, axis, size):
    step = 1
    while step < size:
        value = value + lax.ppermute(value, axis, [(n, n ^ step) for n in range(size)])
        step *= 2
    return value


def general(spectra, hour_flags, sources, station_rows):
    me = lax.axis_index("sta")
    values = spectra[0].astype(F32)
    power = jnp.mean(values * values, axis=(2, 3))
    valid = hour_flags[0].astype(F32)
    white = (values * (valid / jnp.sqrt(power + EPSILON))[:, :, None, None]).astype(BF16)
    white = white.reshape(16, 16, BINS).transpose(1, 0, 2)
    rows = station_rows[sources.reshape(-1)]
    holder, local = rows // 16, rows % 16
    mine = (holder == me)[:, None]
    source_valid = sum_over(jnp.where(mine, valid[local], 0.0), "sta", 32)
    shared = jnp.dot(source_valid, valid.T, precision=lax.Precision.HIGHEST)
    weights = (1.0 / jnp.maximum(shared, 1.0)).reshape(256, 1) * (1.0 / math.sqrt(BINS))
    kept = jnp.where(mine, white[:, local], 0).astype(BF16)
    src = sum_over(kept.reshape(256, BINS), "sta", 32)
    term = correlate(white.reshape(256, BINS), src, weights).astype(F32)
    term = sum_over(term, "day", 8)
    return lax.dynamic_slice_in_dim(term, 128 * lax.axis_index("day"), 128, 1)


def shards(spectra, hour_flags, sources, station_rows):
    stacked, load = fused(sources, station_rows, spectra[0], hour_flags)
    stacked = lax.cond(
        load[0] <= SLOTS,
        lambda *args: stacked,
        general,
        spectra, hour_flags, sources, station_rows,
    )
    return stacked.reshape(16, 16, 128)


def solution(mesh):
    in_specs = (P("day", "sta", None, None, None), P("day", "sta", None), P(), P())
    out_specs = P(None, "sta", "day")
    return jax.shard_map(shards, mesh=mesh, in_specs=in_specs, out_specs=out_specs, check_vma=False)
```

```python
import functools
import math

import jax
import jax.numpy as jnp
import ml_dtypes
import numpy as np
from jax import lax
from jax.experimental import pallas as pl
from jax.experimental.pallas import tpu as pltpu
from jax.sharding import PartitionSpec as P

BINS = 3584
LAGS = 1024
HALF = LAGS // 2
QUARTER = BINS // 4
EPSILON = 1e-06
SLOTS = 4
PARTS = ((0, 384), (384, 512))
MESH = pl.DeviceIdType.MESH
BF16 = jnp.bfloat16
F32 = jnp.float32


def tables():
    bins = np.arange(BINS, dtype=np.int64)[:, None]
    half_lags = 2 * np.arange(HALF, dtype=np.int64)[None] + 1
    angles = np.pi * ((bins * half_lags) % (4 * BINS)) / (2 * BINS)
    table = np.concatenate([np.cos(angles), np.sin(angles)], 1).astype(ml_dtypes.bfloat16)
    shift = np.pi * np.arange(BINS) / (2 * BINS)
    turn = np.stack([np.cos(shift), np.sin(shift)]).astype(np.float32)
    mirror = np.eye(HALF)[::-1].astype(ml_dtypes.bfloat16)
    return table, turn, mirror


def mult(value, k):
    return pl.multiple_of(value, k)


def correlate_kernel(white, src, table, turn, mirror, weights, out, cross, total, rec_f, src_f):
    step = pl.program_id(0)
    tiles = white.shape[1] // 128

    @pl.when(step == 0)
    def _():
        total[...] = jnp.zeros_like(total)

    for t in range(tiles):
        lanes = pl.ds(t * 128, 128)
        co, si = turn[0:1, lanes], turn[1:2, lanes]
        for h in range(8):
            c = white[pl.ds(32 * h, 16), lanes].astype(F32)
            e = white[pl.ds(32 * h + 16, 16), lanes].astype(F32)
            rec_f[t, h, 0], rec_f[t, h, 1], rec_f[t, h, 2] = c, c - e, c + e
            a = src[pl.ds(32 * h, 16), lanes].astype(F32)
            b = src[pl.ds(32 * h + 16, 16), lanes].astype(F32)
            a_turn, b_turn = a * co + b * si, b * co - a * si
            src_f[t, h, 0], src_f[t, h, 1], src_f[t, h, 2] = a_turn + b_turn, b_turn, a_turn
    for t in range(tiles):
        lanes = pl.ds(t * 128, 128)
        for block in range(4):
            sums = [[None] * 3 for _ in range(4)]
            for h in range(8):
                rec = [rec_f[t, h, k] for k in range(3)]
                for n in range(4):
                    for k in range(3):
                        row = src_f[t, h, k, pl.ds(block * 4 + n, 1), :]
                        term = jnp.broadcast_to(row, (16, 128)) * rec[k]
                        sums[n][k] = term if h == 0 else sums[n][k] + term
            for n in range(4):
                rows = pl.ds(16 * (block * 4 + n), 16)
                cross[0, rows, lanes] = (sums[n][0] - sums[n][1]).astype(BF16)
                cross[1, rows, lanes] = (sums[n][0] - sums[n][2]).astype(BF16)
    total[0] += jnp.dot(cross[0], table[:, 0:HALF], preferred_element_type=F32)
    total[1] += jnp.dot(cross[1], table[:, HALF:], preferred_element_type=F32)

    @pl.when(step == pl.num_programs(0) - 1)
    def _():
        scale = weights[...]
        even, odd = total[0] * scale, total[1] * scale
        out[:, HALF:] = (even - odd).astype(BF16)
        back = jnp.dot((even + odd).astype(BF16), mirror[...], preferred_element_type=F32)
        out[:, 0:HALF] = back.astype(BF16)


def correlate(white, src, weights):
    table, turn, mirror = tables()
    width = QUARTER
    return pl.pallas_call(
        correlate_kernel,
        grid=(BINS // width,),
        out_shape=jax.ShapeDtypeStruct((256, LAGS), BF16),
        in_specs=[
            pl.BlockSpec((256, width), lambda q: (0, q)),
            pl.BlockSpec((256, width), lambda q: (0, q)),
            pl.BlockSpec((width, LAGS), lambda q: (q, 0)),
            pl.BlockSpec((2, width), lambda q: (0, q)),
            pl.BlockSpec((HALF, HALF), lambda q: (0, 0)),
            pl.BlockSpec((256, 1), lambda q: (0, 0)),
        ],
        out_specs=pl.BlockSpec((256, LAGS), lambda q: (0, 0)),
        scratch_shapes=[
            pltpu.VMEM((2, 256, width), BF16),
            pltpu.VMEM((2, 256, HALF), F32),
            pltpu.VMEM((width // 128, 8, 3, 16, 128), F32),
            pltpu.VMEM((width // 128, 8, 3, 16, 128), F32),
        ],
        compiler_params=pltpu.CompilerParams(vmem_limit_bytes=48 << 20),
    )(white, src, jnp.asarray(table), jnp.asarray(turn), jnp.asarray(mirror), weights)


def fused_kernel(sources, rows_ref, spectra_hbm, flags, table_hbm, turn, mirror, out, load, spectra, table, white, slots, recv, picked,
                 twin, src, valid, cross, total, rec_f, src_f, scale_ref, days, daily, s_spec, s_tab, s_sc, r_sc, s_tw, r_tw, s_z, r_z,
                 s_x, r_x, s_t, r_t, s_fz, r_fz, s_fx, r_fx, s_ft, r_ft, s_d, r_d):
    day = lax.axis_index("day")
    me = lax.axis_index("sta")
    z, x, c, chip = me // 8, (me // 2) % 4, me % 2, me // 2

    def dev(z_to, x_to, c_to):
        return (day, z_to * 8 + x_to * 2 + c_to)

    def remote(source, target, s_sem, r_sem, device):
        copy = pltpu.make_async_remote_copy(
            src_ref=source, dst_ref=target, send_sem=s_sem, recv_sem=r_sem, device_id=device, device_id_type=MESH
        )
        copy.start()
        return copy

    spectra_copy = pltpu.make_async_copy(spectra_hbm, spectra, s_spec)
    spectra_copy.start()
    offsets = [(dz, dx) for dz in (2, 1, 3, 0) for dx in (2, 1, 3, 0) if (dz, dx) != (0, 0)]
    barrier = pltpu.get_barrier_semaphore()
    for dz, dx in offsets:
        pl.semaphore_signal(barrier, inc=1, device_id=dev((z + dz) % 4, (x + dx) % 4, c), device_id_type=MESH)
    pl.semaphore_signal(barrier, inc=1, device_id=dev(z, x, 1 - c), device_id_type=MESH)
    for n in range(1, 8):
        pl.semaphore_signal(barrier, inc=1, device_id=((day + n) % 8, me), device_id_type=MESH)
    table_copy = pltpu.make_async_copy(table_hbm, table, s_tab)
    table_copy.start()

    ri = lax.broadcasted_iota(jnp.int32, (256, 256), 0)
    ci = lax.broadcasted_iota(jnp.int32, (256, 256), 1)
    natural = (ri % 16) * 16 + 4 * ((ri // 32) % 4) + 2 * (ri // 128) + (ri // 16) % 2
    order = jnp.where(ci == natural, 1.0, 0.0).astype(BF16)
    power = jnp.zeros((256, 128), F32)
    spectra_copy.wait()
    for k in range(BINS // 256):
        lanes = pl.ds(256 * k, 256)
        values = jnp.dot(order, spectra[:, :, :, lanes].reshape(256, 256), preferred_element_type=F32)
        white[:, lanes] = values.astype(BF16)
        squares = values * values
        power = power + squares[:, :128] + squares[:, 128:]
    power = jnp.sum(power, axis=1, keepdims=True)
    flag = flags[0].astype(F32)
    for h in range(8):
        hour = 2 * (h % 4) + h // 4
        mean = (power[32 * h:32 * h + 16] + power[32 * h + 16:32 * h + 32]) * (1.0 / (2 * BINS))
        scale = flag[:, hour:hour + 1] / jnp.sqrt(mean + EPSILON)
        for p in range(2):
            rows = pl.ds(32 * h + 16 * p, 16)
            white[rows, :] = (white[rows, :].astype(F32) * scale).astype(BF16)
    wide = jnp.concatenate([flag, jnp.zeros((16, 120), F32)], axis=1)
    own_flags = pl.ds(mult(256 * c + 64 * x + 16 * z, 16), 16)
    valid[own_flags, :] = wide.astype(BF16)

    holder, local, rank = [], [], []
    most = jnp.int32(0)
    for i in range(16):
        row = rows_ref[sources[i // 8, i % 8]]
        holder.append(row // 16)
        local.append(row % 16)
        count = jnp.int32(0)
        for j in range(i):
            count = count + jnp.where(holder[j] == holder[i], 1, 0)
        rank.append(count)
        most = jnp.maximum(most, count + 1)
    load[0] = most
    ri, ci = ri[:64], ci[:64]
    target = jnp.full((64, 256), -1, jnp.int32)
    base = 128 * ((ri // 8) % 2) + 32 * (ri // 16) + 16 * ((ri // 4) % 2)
    for i in range(16):
        key = jnp.where(holder[i] == me, rank[i], 99)
        target = jnp.where(ri % 4 == key, base + local[i], target)
    pick = jnp.where(ci == target, 1.0, 0.0).astype(BF16)
    slots[...] = jnp.dot(pick, white[...], preferred_element_type=F32).astype(BF16)
    pl.semaphore_wait(barrier, 23)

    def lanes_of(x_of, part):
        start, width = PARTS[part]
        return pl.ds(mult(QUARTER * x_of + start, 128), width)

    scattered = []
    for part, (start, width) in enumerate(PARTS):
        copies = []
        for n, (dz, dx) in enumerate(offsets):
            z_to, x_to = (z + dz) % 4, (x + dx) % 4
            copies.append(
                remote(
                    slots.at[pl.ds(mult(16 * z_to, 16), 16), lanes_of(x_to, part)],
                    recv.at[pl.ds(mult(16 * chip, 16), 16), pl.ds(start, width)],
                    s_sc.at[part, n],
                    r_sc.at[part, n],
                    dev(z_to, x_to, c),
                )
            )
        scattered.append(copies)
    ref = valid.at[own_flags]
    flag_z = [remote(ref, ref, s_fz.at[n], r_fz.at[n], dev((z + 1 + n) % 4, x, c)) for n in range(3)]
    recv[pl.ds(mult(16 * chip, 16), 16), :] = slots[
        pl.ds(mult(16 * z, 16), 16), pl.ds(mult(QUARTER * x, 128), QUARTER)
    ]
    target = jnp.full((64, 256), -1, jnp.int32)
    for i in range(16):
        where = jnp.where(holder[i] % 2 == c, 16 * (holder[i] // 2) + rank[i], -1000)
        target = jnp.where(ri % 16 == i, where + 8 * (ri // 32) + 4 * ((ri // 16) % 2), target)
    pick = jnp.where(ci == target, 1.0, 0.0).astype(BF16)

    def receiver_planes(t, carry):
        lanes = pl.ds(mult(t * 128, 128), 128)
        for h in range(8):
            cosine = white[pl.ds(32 * h, 16), lanes].astype(F32)
            sine = white[pl.ds(32 * h + 16, 16), lanes].astype(F32)
            rec_f[t, h, 0] = cosine
            rec_f[t, h, 1] = cosine - sine
            rec_f[t, h, 2] = cosine + sine
        return carry

    lax.fori_loop(0, BINS // 128, receiver_planes, 0)
    total[...] = jnp.zeros_like(total)

    def piece(z_of, x_of, part):
        return src.at[pl.ds(mult(128 * c + 32 * z_of, 32), 32), lanes_of(x_of, part)]

    def send(ref, s_sem, r_sem, device):
        return remote(ref, ref, s_sem, r_sem, device)

    def send_x(part, k, z_of):
        ref = piece(z_of, x, part)
        return [
            send(ref, s_x.at[part, k, n], r_x.at[part, k, n], dev(z, (x + dx) % 4, c))
            for n, dx in enumerate((2, 1, 3))
        ]

    def send_across(part, n, x_of):
        ref = src.at[pl.ds(mult(128 * c, 128), 128), lanes_of(x_of, part)]
        return send(ref, s_t.at[part, n], r_t.at[part, n], dev(z, x, 1 - c))

    along_z, along_x, across = [], [], []
    for part, (start, width) in enumerate(PARTS):
        for copy in scattered[part]:
            copy.wait()
        here = pl.ds(start, width)
        picked[:, here] = jnp.dot(pick, recv[:, here], preferred_element_type=F32).astype(BF16)
        copy = remote(
            picked.at[pl.ds(mult(32 * (1 - c), 32), 32), here],
            twin.at[:, here],
            s_tw.at[part],
            r_tw.at[part],
            dev(z, x, 1 - c),
        )
        if part == 0:
            for other in flag_z:
                other.wait()
            ref = valid.at[pl.ds(mult(256 * c + 64 * x, 64), 64)]
            flag_x = [remote(ref, ref, s_fx.at[n], r_fx.at[n], dev(z, (x + 1 + n) % 4, c)) for n in range(3)]
        copy.wait()
        ref = piece(z, x, part)
        ref[...] = picked[pl.ds(mult(32 * c, 32), 32), here] + twin[:, here]
        along_z.append(
            [
                send(ref, s_z.at[part, n], r_z.at[part, n], dev((z + dz) % 4, x, c))
                for n, dz in enumerate((2, 1, 3))
            ]
        )
        along_x.append([send_x(part, 0, z)])
    def products(q, part, into, blocks, keep, fresh):
        start, width = PARTS[part]

        def tile(t, carry):
            all_lanes = pl.ds(mult(QUARTER * q + start + 128 * t, 128), 128)
            lanes = pl.ds(mult(128 * t, 128), 128)
            at = 7 * q + start // 128 + t
            if fresh:
                co, si = turn[0:1, all_lanes], turn[1:2, all_lanes]
                for h in range(8):
                    a = src[pl.ds(32 * h, 16), all_lanes].astype(F32)
                    b = src[pl.ds(32 * h + 16, 16), all_lanes].astype(F32)
                    a_turn, b_turn = a * co + b * si, b * co - a * si
                    src_f[keep + t, h, 0] = a_turn + b_turn
                    src_f[keep + t, h, 1] = b_turn
                    src_f[keep + t, h, 2] = a_turn
            for block in blocks:
                sums = [[None] * 3 for _ in range(4)]
                for h in range(8):
                    rec = [rec_f[at, h, k] for k in range(3)]
                    for n in range(4):
                        for k in range(3):
                            row = src_f[keep + t, h, k, pl.ds(block * 4 + n, 1), :]
                            term = jnp.broadcast_to(row, (16, 128)) * rec[k]
                            sums[n][k] = term if h == 0 else sums[n][k] + term
                for n in range(4):
                    rows = pl.ds(16 * (block * 4 + n), 16)
                    cross[into, 0, rows, lanes] = (sums[n][0] - sums[n][1]).astype(BF16)
                    cross[into, 1, rows, lanes] = (sums[n][0] - sums[n][2]).astype(BF16)
            return carry

        lax.fori_loop(0, width // 128, tile, 0)

    def to_lags(q, part, into, rows):
        start, width = PARTS[part]
        bins = lanes_of(q, part)
        total[0, rows] += jnp.dot(cross[into, 0, rows, 0:width], table[bins, 0:HALF], preferred_element_type=F32)
        total[1, rows] += jnp.dot(cross[into, 1, rows, 0:width], table[bins, HALF:], preferred_element_type=F32)

    def correlate_part(q, part):
        products(q, part, 0, range(4), 0, True)
        to_lags(q, part, 0, pl.ds(0, 256))

    def take_x(part, n, dx):
        for k in range(4):
            along_x[part][k][n].wait()
        across[part].append(send_across(part, 1 + n, (x + 4 - dx) % 4))

    for copy in flag_x:
        copy.wait()
    ref = valid.at[pl.ds(mult(256 * c, 256), 256)]
    flag_t = remote(ref, ref, s_ft, r_ft, dev(z, x, 1 - c))
    flag_t.wait()
    ri = lax.broadcasted_iota(jnp.int32, (256, 512), 0)
    ci = lax.broadcasted_iota(jnp.int32, (256, 512), 1)
    target = jnp.full((256, 512), -1, jnp.int32)
    for i in range(16):
        where = 256 * (holder[i] % 2) + 64 * ((holder[i] // 2) % 4) + 16 * (holder[i] // 8) + local[i]
        target = jnp.where(ri // 16 == i, where, target)
    choose = jnp.where(ci == target, 1.0, 0.0).astype(BF16)
    shared = jnp.dot(choose, valid[...], preferred_element_type=F32) * jnp.concatenate([wide] * 16, axis=0)
    shared = jnp.sum(shared, axis=1, keepdims=True)
    scale_ref[...] = (1.0 / jnp.maximum(shared, 1.0)) * (1.0 / math.sqrt(BINS))

    def take_z(part):
        for n, dz in ((1, 1), (2, 3), (0, 2)):
            along_z[part][n].wait()
            along_x[part].append(send_x(part, 1 + n, (z + 4 - dz) % 4))
        across.append([send_across(part, 0, x)])

    table_copy.wait()
    take_z(0)
    across[0][0].wait()
    correlate_part(x, 0)
    take_z(1)
    for n, dx in ((1, 1), (2, 3)):
        take_x(0, n, dx)
    across[1][0].wait()
    correlate_part(x, 1)
    take_x(0, 0, 2)
    across[0][1].wait()
    correlate_part((x + 3) % 4, 0)
    across[0][2].wait()
    correlate_part((x + 1) % 4, 0)
    across[0][3].wait()
    correlate_part((x + 2) % 4, 0)
    for n, dx in ((1, 1), (2, 3), (0, 2)):
        take_x(1, n, dx)
    copies = []
    for half in range(2):
        rows = pl.ds(128 * half, 128)
        for n, dx in enumerate((3, 1, 2)):
            if half == 0:
                across[1][1 + n].wait()
            products((x + dx) % 4, 1, n, range(2 * half, 2 * half + 2), 4 * n, half == 0)
        for n, dx in enumerate((3, 1, 2)):
            to_lags((x + dx) % 4, 1, n, rows)
        even, odd = total[0, rows] * scale_ref[rows, :], total[1, rows] * scale_ref[rows, :]
        for n in range(4):
            daily[4 + n, rows] = (even - odd)[:, 128 * n:128 * n + 128].astype(BF16)
        back = jnp.dot((even + odd).astype(BF16), mirror[...], preferred_element_type=F32)
        for n in range(4):
            daily[n, rows] = back[:, 128 * n:128 * n + 128].astype(BF16)
        for n in (4, 3, 5, 2, 6, 1, 7):
            to = (day + n) % 8
            copies.append(
                remote(
                    daily.at[to, rows],
                    days.at[n - 1, rows],
                    s_d.at[half, n - 1],
                    r_d.at[half, n - 1],
                    (to, me),
                )
            )
    for copy in copies:
        copy.wait()
    result = daily[day].astype(F32)
    for n in range(7):
        result = result + days[n].astype(F32)
    out[...] = result


def fused(sources, station_rows, spectra, flags):
    table, turn, mirror = tables()
    sem = pltpu.SemaphoreType.DMA
    vmem = pl.BlockSpec(memory_space=pltpu.VMEM)
    smem = pl.BlockSpec(memory_space=pltpu.SMEM)
    hbm = pl.BlockSpec(memory_space=pl.ANY)
    return pl.pallas_call(
        fused_kernel,
        out_shape=(jax.ShapeDtypeStruct((256, 128), F32), jax.ShapeDtypeStruct((1,), jnp.int32)),
        in_specs=[smem, smem, hbm, vmem, hbm, vmem, vmem],
        out_specs=(vmem, smem),
        scratch_shapes=[
            pltpu.VMEM((16, 8, 2, BINS), BF16),
            pltpu.VMEM((BINS, LAGS), BF16),
            pltpu.VMEM((256, BINS), BF16),
            pltpu.VMEM((64, BINS), BF16),
            pltpu.VMEM((256, QUARTER), BF16),
            pltpu.VMEM((64, QUARTER), BF16),
            pltpu.VMEM((32, QUARTER), BF16),
            pltpu.VMEM((256, BINS), BF16),
            pltpu.VMEM((512, 128), BF16),
            pltpu.VMEM((3, 2, 256, 512), BF16),
            pltpu.VMEM((2, 256, HALF), F32),
            pltpu.VMEM((BINS // 128, 8, 3, 16, 128), F32),
            pltpu.VMEM((12, 8, 3, 16, 128), F32),
            pltpu.VMEM((256, 1), F32),
            pltpu.VMEM((7, 256, 128), BF16),
            pltpu.VMEM((8, 256, 128), BF16),
            sem, sem,
            sem((2, 15)), sem((2, 15)), sem((2,)), sem((2,)), sem((2, 3)), sem((2, 3)), sem((2, 4, 3)), sem((2, 4, 3)),
            sem((2, 4)), sem((2, 4)),
            sem((3,)), sem((3,)), sem((3,)), sem((3,)), sem, sem, sem((2, 7)), sem((2, 7)),
        ],
        compiler_params=pltpu.CompilerParams(collective_id=0, has_side_effects=True, vmem_limit_bytes=52 << 20),
    )(sources, station_rows, spectra, flags, jnp.asarray(table), jnp.asarray(turn), jnp.asarray(mirror))


def sum_over(value, axis, size):
    step = 1
    while step < size:
        value = value + lax.ppermute(value, axis, [(n, n ^ step) for n in range(size)])
        step *= 2
    return value


def general(spectra, hour_flags, sources, station_rows):
    me = lax.axis_index("sta")
    values = spectra[0].astype(F32)
    power = jnp.mean(values * values, axis=(2, 3))
    valid = hour_flags[0].astype(F32)
    white = (values * (valid / jnp.sqrt(power + EPSILON))[:, :, None, None]).astype(BF16)
    white = white.reshape(16, 16, BINS).transpose(1, 0, 2)
    rows = station_rows[sources.reshape(-1)]
    holder, local = rows // 16, rows % 16
    mine = (holder == me)[:, None]
    source_valid = sum_over(jnp.where(mine, valid[local], 0.0), "sta", 32)
    shared = jnp.dot(source_valid, valid.T, precision=lax.Precision.HIGHEST)
    weights = (1.0 / jnp.maximum(shared, 1.0)).reshape(256, 1) * (1.0 / math.sqrt(BINS))
    kept = jnp.where(mine, white[:, local], 0).astype(BF16)
    src = sum_over(kept.reshape(256, BINS), "sta", 32)
    term = correlate(white.reshape(256, BINS), src, weights).astype(F32)
    term = sum_over(term, "day", 8)
    return lax.dynamic_slice_in_dim(term, 128 * lax.axis_index("day"), 128, 1)


def shards(spectra, hour_flags, sources, station_rows):
    stacked, load = fused(sources, station_rows, spectra[0], hour_flags)
    stacked = lax.cond(
        load[0] <= SLOTS,
        lambda *args: stacked,
        general,
        spectra, hour_flags, sources, station_rows,
    )
    return stacked.reshape(16, 16, 128)


def solution(mesh):
    in_specs = (P("day", "sta", None, None, None), P("day", "sta", None), P(), P())
    out_specs = P(None, "sta", "day")
    return jax.shard_map(shards, mesh=mesh, in_specs=in_specs, out_specs=out_specs, check_vma=False)
```

```python
import functools
import math

import jax
import jax.numpy as jnp
import ml_dtypes
import numpy as np
from jax import lax
from jax.experimental import pallas as pl
from jax.experimental.pallas import tpu as pltpu
from jax.sharding import PartitionSpec as P

BINS = 3584
LAGS = 1024
HALF = LAGS // 2
QUARTER = BINS // 4
EPSILON = 1e-06
SLOTS = 4
PARTS = ((0, 384), (384, 512))
MESH = pl.DeviceIdType.MESH
BF16 = jnp.bfloat16
F32 = jnp.float32


def tables():
    bins = np.arange(BINS, dtype=np.int64)[:, None]
    half_lags = 2 * np.arange(HALF, dtype=np.int64)[None] + 1
    angles = np.pi * ((bins * half_lags) % (4 * BINS)) / (2 * BINS)
    table = np.concatenate([np.cos(angles), np.sin(angles)], 1).astype(ml_dtypes.bfloat16)
    shift = np.pi * np.arange(BINS) / (2 * BINS)
    turn = np.stack([np.cos(shift), np.sin(shift)]).astype(np.float32)
    mirror = np.eye(HALF)[::-1].astype(ml_dtypes.bfloat16)
    return table, turn, mirror


def mult(value, k):
    return pl.multiple_of(value, k)


def correlate_kernel(white, src, table, turn, mirror, weights, out, cross, total, rec_f, src_f):
    step = pl.program_id(0)
    tiles = white.shape[1] // 128

    @pl.when(step == 0)
    def _():
        total[...] = jnp.zeros_like(total)

    for t in range(tiles):
        lanes = pl.ds(t * 128, 128)
        co, si = turn[0:1, lanes], turn[1:2, lanes]
        for h in range(8):
            c = white[pl.ds(32 * h, 16), lanes].astype(F32)
            e = white[pl.ds(32 * h + 16, 16), lanes].astype(F32)
            rec_f[t, h, 0], rec_f[t, h, 1], rec_f[t, h, 2] = c, c - e, c + e
            a = src[pl.ds(32 * h, 16), lanes].astype(F32)
            b = src[pl.ds(32 * h + 16, 16), lanes].astype(F32)
            a_turn, b_turn = a * co + b * si, b * co - a * si
            src_f[t, h, 0], src_f[t, h, 1], src_f[t, h, 2] = a_turn + b_turn, b_turn, a_turn
    for t in range(tiles):
        lanes = pl.ds(t * 128, 128)
        for block in range(4):
            sums = [[None] * 3 for _ in range(4)]
            for h in range(8):
                rec = [rec_f[t, h, k] for k in range(3)]
                for n in range(4):
                    for k in range(3):
                        row = src_f[t, h, k, pl.ds(block * 4 + n, 1), :]
                        term = jnp.broadcast_to(row, (16, 128)) * rec[k]
                        sums[n][k] = term if h == 0 else sums[n][k] + term
            for n in range(4):
                rows = pl.ds(16 * (block * 4 + n), 16)
                cross[0, rows, lanes] = (sums[n][0] - sums[n][1]).astype(BF16)
                cross[1, rows, lanes] = (sums[n][0] - sums[n][2]).astype(BF16)
    total[0] += jnp.dot(cross[0], table[:, 0:HALF], preferred_element_type=F32)
    total[1] += jnp.dot(cross[1], table[:, HALF:], preferred_element_type=F32)

    @pl.when(step == pl.num_programs(0) - 1)
    def _():
        scale = weights[...]
        even, odd = total[0] * scale, total[1] * scale
        out[:, HALF:] = (even - odd).astype(BF16)
        back = jnp.dot((even + odd).astype(BF16), mirror[...], preferred_element_type=F32)
        out[:, 0:HALF] = back.astype(BF16)


def correlate(white, src, weights):
    table, turn, mirror = tables()
    width = QUARTER
    return pl.pallas_call(
        correlate_kernel,
        grid=(BINS // width,),
        out_shape=jax.ShapeDtypeStruct((256, LAGS), BF16),
        in_specs=[
            pl.BlockSpec((256, width), lambda q: (0, q)),
            pl.BlockSpec((256, width), lambda q: (0, q)),
            pl.BlockSpec((width, LAGS), lambda q: (q, 0)),
            pl.BlockSpec((2, width), lambda q: (0, q)),
            pl.BlockSpec((HALF, HALF), lambda q: (0, 0)),
            pl.BlockSpec((256, 1), lambda q: (0, 0)),
        ],
        out_specs=pl.BlockSpec((256, LAGS), lambda q: (0, 0)),
        scratch_shapes=[
            pltpu.VMEM((2, 256, width), BF16),
            pltpu.VMEM((2, 256, HALF), F32),
            pltpu.VMEM((width // 128, 8, 3, 16, 128), F32),
            pltpu.VMEM((width // 128, 8, 3, 16, 128), F32),
        ],
        compiler_params=pltpu.CompilerParams(vmem_limit_bytes=48 << 20),
    )(white, src, jnp.asarray(table), jnp.asarray(turn), jnp.asarray(mirror), weights)


def fused_kernel(sources, rows_ref, spectra_hbm, flags, table_hbm, turn, mirror, out, load, spectra, table, white, slots, recv, picked,
                 twin, src, valid, cross, total, rec_f, src_f, scale_ref, days, daily, s_spec, s_tab, s_sc, r_sc, s_tw, r_tw, s_z, r_z,
                 s_x, r_x, s_t, r_t, s_fz, r_fz, s_fx, r_fx, s_ft, r_ft, s_d, r_d):
    day = lax.axis_index("day")
    me = lax.axis_index("sta")
    z, x, c, chip = me // 8, (me // 2) % 4, me % 2, me // 2

    def dev(z_to, x_to, c_to):
        return (day, z_to * 8 + x_to * 2 + c_to)

    def remote(source, target, s_sem, r_sem, device):
        copy = pltpu.make_async_remote_copy(
            src_ref=source, dst_ref=target, send_sem=s_sem, recv_sem=r_sem, device_id=device, device_id_type=MESH
        )
        copy.start()
        return copy

    spectra_copy = pltpu.make_async_copy(spectra_hbm, spectra, s_spec)
    spectra_copy.start()
    offsets = [(dz, dx) for dz in (2, 1, 3, 0) for dx in (2, 1, 3, 0) if (dz, dx) != (0, 0)]
    barrier = pltpu.get_barrier_semaphore()
    for dz, dx in offsets:
        pl.semaphore_signal(barrier, inc=1, device_id=dev((z + dz) % 4, (x + dx) % 4, c), device_id_type=MESH)
    pl.semaphore_signal(barrier, inc=1, device_id=dev(z, x, 1 - c), device_id_type=MESH)
    for n in range(1, 8):
        pl.semaphore_signal(barrier, inc=1, device_id=((day + n) % 8, me), device_id_type=MESH)
    table_copy = pltpu.make_async_copy(table_hbm, table, s_tab)
    table_copy.start()

    ri = lax.broadcasted_iota(jnp.int32, (256, 256), 0)
    ci = lax.broadcasted_iota(jnp.int32, (256, 256), 1)
    natural = (ri % 16) * 16 + 4 * ((ri // 32) % 4) + 2 * (ri // 128) + (ri // 16) % 2
    order = jnp.where(ci == natural, 1.0, 0.0).astype(BF16)
    power = jnp.zeros((256, 128), F32)
    spectra_copy.wait()
    for k in range(BINS // 256):
        lanes = pl.ds(256 * k, 256)
        values = jnp.dot(order, spectra[:, :, :, lanes].reshape(256, 256), preferred_element_type=F32)
        white[:, lanes] = values.astype(BF16)
        squares = values * values
        power = power + squares[:, :128] + squares[:, 128:]
    power = jnp.sum(power, axis=1, keepdims=True)
    flag = flags[0].astype(F32)
    for h in range(8):
        hour = 2 * (h % 4) + h // 4
        mean = (power[32 * h:32 * h + 16] + power[32 * h + 16:32 * h + 32]) * (1.0 / (2 * BINS))
        scale = flag[:, hour:hour + 1] / jnp.sqrt(mean + EPSILON)
        for p in range(2):
            rows = pl.ds(32 * h + 16 * p, 16)
            white[rows, :] = (white[rows, :].astype(F32) * scale).astype(BF16)
    wide = jnp.concatenate([flag, jnp.zeros((16, 120), F32)], axis=1)
    own_flags = pl.ds(mult(256 * c + 64 * x + 16 * z, 16), 16)
    valid[own_flags, :] = wide.astype(BF16)

    holder, local, rank = [], [], []
    most = jnp.int32(0)
    for i in range(16):
        row = rows_ref[sources[i // 8, i % 8]]
        holder.append(row // 16)
        local.append(row % 16)
        count = jnp.int32(0)
        for j in range(i):
            count = count + jnp.where(holder[j] == holder[i], 1, 0)
        rank.append(count)
        most = jnp.maximum(most, count + 1)
    load[0] = most
    ri, ci = ri[:64], ci[:64]
    target = jnp.full((64, 256), -1, jnp.int32)
    base = 128 * ((ri // 8) % 2) + 32 * (ri // 16) + 16 * ((ri // 4) % 2)
    for i in range(16):
        key = jnp.where(holder[i] == me, rank[i], 99)
        target = jnp.where(ri % 4 == key, base + local[i], target)
    pick = jnp.where(ci == target, 1.0, 0.0).astype(BF16)
    slots[...] = jnp.dot(pick, white[...], preferred_element_type=F32).astype(BF16)
    pl.semaphore_wait(barrier, 23)

    def lanes_of(x_of, part):
        start, width = PARTS[part]
        return pl.ds(mult(QUARTER * x_of + start, 128), width)

    scattered = []
    for part, (start, width) in enumerate(PARTS):
        copies = []
        for n, (dz, dx) in enumerate(offsets):
            z_to, x_to = (z + dz) % 4, (x + dx) % 4
            copies.append(
                remote(
                    slots.at[pl.ds(mult(16 * z_to, 16), 16), lanes_of(x_to, part)],
                    recv.at[pl.ds(mult(16 * chip, 16), 16), pl.ds(start, width)],
                    s_sc.at[part, n],
                    r_sc.at[part, n],
                    dev(z_to, x_to, c),
                )
            )
        scattered.append(copies)
    ref = valid.at[own_flags]
    flag_z = [remote(ref, ref, s_fz.at[n], r_fz.at[n], dev((z + 1 + n) % 4, x, c)) for n in range(3)]
    recv[pl.ds(mult(16 * chip, 16), 16), :] = slots[
        pl.ds(mult(16 * z, 16), 16), pl.ds(mult(QUARTER * x, 128), QUARTER)
    ]
    target = jnp.full((64, 256), -1, jnp.int32)
    for i in range(16):
        where = jnp.where(holder[i] % 2 == c, 16 * (holder[i] // 2) + rank[i], -1000)
        target = jnp.where(ri % 16 == i, where + 8 * (ri // 32) + 4 * ((ri // 16) % 2), target)
    pick = jnp.where(ci == target, 1.0, 0.0).astype(BF16)

    def receiver_planes(t, carry):
        lanes = pl.ds(mult(t * 128, 128), 128)
        for h in range(8):
            cosine = white[pl.ds(32 * h, 16), lanes].astype(F32)
            sine = white[pl.ds(32 * h + 16, 16), lanes].astype(F32)
            rec_f[t, h, 0] = cosine
            rec_f[t, h, 1] = cosine - sine
            rec_f[t, h, 2] = cosine + sine
        return carry

    lax.fori_loop(0, BINS // 128, receiver_planes, 0)
    total[...] = jnp.zeros_like(total)

    def piece(z_of, x_of, part):
        return src.at[pl.ds(mult(128 * c + 32 * z_of, 32), 32), lanes_of(x_of, part)]

    def send(ref, s_sem, r_sem, device):
        return remote(ref, ref, s_sem, r_sem, device)

    def send_x(part, k, z_of):
        ref = piece(z_of, x, part)
        return [
            send(ref, s_x.at[part, k, n], r_x.at[part, k, n], dev(z, (x + dx) % 4, c))
            for n, dx in enumerate((2, 1, 3))
        ]

    def send_across(part, n, x_of):
        ref = src.at[pl.ds(mult(128 * c, 128), 128), lanes_of(x_of, part)]
        return send(ref, s_t.at[part, n], r_t.at[part, n], dev(z, x, 1 - c))

    along_z, along_x, across = [], [], []
    for part, (start, width) in enumerate(PARTS):
        for copy in scattered[part]:
            copy.wait()
        here = pl.ds(start, width)
        picked[:, here] = jnp.dot(pick, recv[:, here], preferred_element_type=F32).astype(BF16)
        copy = remote(
            picked.at[pl.ds(mult(32 * (1 - c), 32), 32), here],
            twin.at[:, here],
            s_tw.at[part],
            r_tw.at[part],
            dev(z, x, 1 - c),
        )
        if part == 0:
            for other in flag_z:
                other.wait()
            ref = valid.at[pl.ds(mult(256 * c + 64 * x, 64), 64)]
            flag_x = [remote(ref, ref, s_fx.at[n], r_fx.at[n], dev(z, (x + 1 + n) % 4, c)) for n in range(3)]
        copy.wait()
        ref = piece(z, x, part)
        ref[...] = picked[pl.ds(mult(32 * c, 32), 32), here] + twin[:, here]
        along_z.append(
            [
                send(ref, s_z.at[part, n], r_z.at[part, n], dev((z + dz) % 4, x, c))
                for n, dz in enumerate((2, 1, 3))
            ]
        )
        along_x.append([send_x(part, 0, z)])
    def products(q, part, into, blocks, keep, fresh):
        start, width = PARTS[part]

        def tile(t, carry):
            all_lanes = pl.ds(mult(QUARTER * q + start + 128 * t, 128), 128)
            lanes = pl.ds(mult(128 * t, 128), 128)
            at = 7 * q + start // 128 + t
            if fresh:
                co, si = turn[0:1, all_lanes], turn[1:2, all_lanes]
                for h in range(8):
                    a = src[pl.ds(32 * h, 16), all_lanes].astype(F32)
                    b = src[pl.ds(32 * h + 16, 16), all_lanes].astype(F32)
                    a_turn, b_turn = a * co + b * si, b * co - a * si
                    src_f[keep + t, h, 0] = a_turn + b_turn
                    src_f[keep + t, h, 1] = b_turn
                    src_f[keep + t, h, 2] = a_turn
            for block in blocks:
                sums = [[None] * 3 for _ in range(4)]
                for h in range(8):
                    rec = [rec_f[at, h, k] for k in range(3)]
                    for n in range(4):
                        for k in range(3):
                            row = src_f[keep + t, h, k, pl.ds(block * 4 + n, 1), :]
                            term = jnp.broadcast_to(row, (16, 128)) * rec[k]
                            sums[n][k] = term if h == 0 else sums[n][k] + term
                for n in range(4):
                    rows = pl.ds(16 * (block * 4 + n), 16)
                    cross[into, 0, rows, lanes] = (sums[n][0] - sums[n][1]).astype(BF16)
                    cross[into, 1, rows, lanes] = (sums[n][0] - sums[n][2]).astype(BF16)
            return carry

        lax.fori_loop(0, width // 128, tile, 0)

    def to_lags(q, part, into, rows):
        start, width = PARTS[part]
        bins = lanes_of(q, part)
        total[0, rows] += jnp.dot(cross[into, 0, rows, 0:width], table[bins, 0:HALF], preferred_element_type=F32)
        total[1, rows] += jnp.dot(cross[into, 1, rows, 0:width], table[bins, HALF:], preferred_element_type=F32)

    def correlate_part(q, part):
        products(q, part, 0, range(4), 0, True)
        to_lags(q, part, 0, pl.ds(0, 256))

    def take_x(part, n, dx):
        for k in range(4):
            along_x[part][k][n].wait()
        across[part].append(send_across(part, 1 + n, (x + 4 - dx) % 4))

    for copy in flag_x:
        copy.wait()
    ref = valid.at[pl.ds(mult(256 * c, 256), 256)]
    flag_t = remote(ref, ref, s_ft, r_ft, dev(z, x, 1 - c))
    flag_t.wait()
    ri = lax.broadcasted_iota(jnp.int32, (256, 512), 0)
    ci = lax.broadcasted_iota(jnp.int32, (256, 512), 1)
    target = jnp.full((256, 512), -1, jnp.int32)
    for i in range(16):
        where = 256 * (holder[i] % 2) + 64 * ((holder[i] // 2) % 4) + 16 * (holder[i] // 8) + local[i]
        target = jnp.where(ri // 16 == i, where, target)
    choose = jnp.where(ci == target, 1.0, 0.0).astype(BF16)
    shared = jnp.dot(choose, valid[...], preferred_element_type=F32) * jnp.concatenate([wide] * 16, axis=0)
    shared = jnp.sum(shared, axis=1, keepdims=True)
    scale_ref[...] = (1.0 / jnp.maximum(shared, 1.0)) * (1.0 / math.sqrt(BINS))

    def take_z(part):
        for n, dz in ((1, 1), (2, 3), (0, 2)):
            along_z[part][n].wait()
            along_x[part].append(send_x(part, 1 + n, (z + 4 - dz) % 4))
        across.append([send_across(part, 0, x)])

    table_copy.wait()
    take_z(0)
    across[0][0].wait()
    correlate_part(x, 0)
    take_z(1)
    for n, dx in ((1, 1), (2, 3)):
        take_x(0, n, dx)
    across[1][0].wait()
    correlate_part(x, 1)
    take_x(0, 0, 2)
    across[0][1].wait()
    correlate_part((x + 3) % 4, 0)
    across[0][2].wait()
    correlate_part((x + 1) % 4, 0)
    for n, dx in ((1, 1), (2, 3)):
        take_x(1, n, dx)
    across[0][3].wait()
    correlate_part((x + 2) % 4, 0)
    take_x(1, 0, 2)
    copies = []
    for half in range(2):
        rows = pl.ds(128 * half, 128)
        for n, dx in enumerate((3, 1, 2)):
            if half == 0:
                across[1][1 + n].wait()
            products((x + dx) % 4, 1, n, range(2 * half, 2 * half + 2), 4 * n, half == 0)
        for n, dx in enumerate((3, 1, 2)):
            to_lags((x + dx) % 4, 1, n, rows)
        even, odd = total[0, rows] * scale_ref[rows, :], total[1, rows] * scale_ref[rows, :]
        for n in range(4):
            daily[4 + n, rows] = (even - odd)[:, 128 * n:128 * n + 128].astype(BF16)
        back = jnp.dot((even + odd).astype(BF16), mirror[...], preferred_element_type=F32)
        for n in range(4):
            daily[n, rows] = back[:, 128 * n:128 * n + 128].astype(BF16)
        for n in (4, 3, 5, 2, 6, 1, 7):
            to = (day + n) % 8
            copies.append(
                remote(
                    daily.at[to, rows],
                    days.at[n - 1, rows],
                    s_d.at[half, n - 1],
                    r_d.at[half, n - 1],
                    (to, me),
                )
            )
    for copy in copies:
        copy.wait()
    result = daily[day].astype(F32)
    for n in range(7):
        result = result + days[n].astype(F32)
    out[...] = result


def fused(sources, station_rows, spectra, flags):
    table, turn, mirror = tables()
    sem = pltpu.SemaphoreType.DMA
    vmem = pl.BlockSpec(memory_space=pltpu.VMEM)
    smem = pl.BlockSpec(memory_space=pltpu.SMEM)
    hbm = pl.BlockSpec(memory_space=pl.ANY)
    return pl.pallas_call(
        fused_kernel,
        out_shape=(jax.ShapeDtypeStruct((256, 128), F32), jax.ShapeDtypeStruct((1,), jnp.int32)),
        in_specs=[smem, smem, hbm, vmem, hbm, vmem, vmem],
        out_specs=(vmem, smem),
        scratch_shapes=[
            pltpu.VMEM((16, 8, 2, BINS), BF16),
            pltpu.VMEM((BINS, LAGS), BF16),
            pltpu.VMEM((256, BINS), BF16),
            pltpu.VMEM((64, BINS), BF16),
            pltpu.VMEM((256, QUARTER), BF16),
            pltpu.VMEM((64, QUARTER), BF16),
            pltpu.VMEM((32, QUARTER), BF16),
            pltpu.VMEM((256, BINS), BF16),
            pltpu.VMEM((512, 128), BF16),
            pltpu.VMEM((3, 2, 256, 512), BF16),
            pltpu.VMEM((2, 256, HALF), F32),
            pltpu.VMEM((BINS // 128, 8, 3, 16, 128), F32),
            pltpu.VMEM((12, 8, 3, 16, 128), F32),
            pltpu.VMEM((256, 1), F32),
            pltpu.VMEM((7, 256, 128), BF16),
            pltpu.VMEM((8, 256, 128), BF16),
            sem, sem,
            sem((2, 15)), sem((2, 15)), sem((2,)), sem((2,)), sem((2, 3)), sem((2, 3)), sem((2, 4, 3)), sem((2, 4, 3)),
            sem((2, 4)), sem((2, 4)),
            sem((3,)), sem((3,)), sem((3,)), sem((3,)), sem, sem, sem((2, 7)), sem((2, 7)),
        ],
        compiler_params=pltpu.CompilerParams(collective_id=0, has_side_effects=True, vmem_limit_bytes=52 << 20),
    )(sources, station_rows, spectra, flags, jnp.asarray(table), jnp.asarray(turn), jnp.asarray(mirror))


def sum_over(value, axis, size):
    step = 1
    while step < size:
        value = value + lax.ppermute(value, axis, [(n, n ^ step) for n in range(size)])
        step *= 2
    return value


def general(spectra, hour_flags, sources, station_rows):
    me = lax.axis_index("sta")
    values = spectra[0].astype(F32)
    power = jnp.mean(values * values, axis=(2, 3))
    valid = hour_flags[0].astype(F32)
    white = (values * (valid / jnp.sqrt(power + EPSILON))[:, :, None, None]).astype(BF16)
    white = white.reshape(16, 16, BINS).transpose(1, 0, 2)
    rows = station_rows[sources.reshape(-1)]
    holder, local = rows // 16, rows % 16
    mine = (holder == me)[:, None]
    source_valid = sum_over(jnp.where(mine, valid[local], 0.0), "sta", 32)
    shared = jnp.dot(source_valid, valid.T, precision=lax.Precision.HIGHEST)
    weights = (1.0 / jnp.maximum(shared, 1.0)).reshape(256, 1) * (1.0 / math.sqrt(BINS))
    kept = jnp.where(mine, white[:, local], 0).astype(BF16)
    src = sum_over(kept.reshape(256, BINS), "sta", 32)
    term = correlate(white.reshape(256, BINS), src, weights).astype(F32)
    term = sum_over(term, "day", 8)
    return lax.dynamic_slice_in_dim(term, 128 * lax.axis_index("day"), 128, 1)


def shards(spectra, hour_flags, sources, station_rows):
    stacked, load = fused(sources, station_rows, spectra[0], hour_flags)
    stacked = lax.cond(
        load[0] <= SLOTS,
        lambda *args: stacked,
        general,
        spectra, hour_flags, sources, station_rows,
    )
    return stacked.reshape(16, 16, 128)


def solution(mesh):
    in_specs = (P("day", "sta", None, None, None), P("day", "sta", None), P(), P())
    out_specs = P(None, "sta", "day")
    return jax.shard_map(shards, mesh=mesh, in_specs=in_specs, out_specs=out_specs, check_vma=False)
```
